128 devices in a mesh: batch: 2 (over core), seq: 8 (over y_lo, x), mp: 8 (over y_hi, z).
Axes of the slice: x: 4, y: 4 (y_hi: 2, y_lo: 2; y = y_hi * 2 + y_lo), z: 4, core: 2. Of those that a mesh axis runs over, the one named last changes fastest.
Arguments:
- inputs: bfloat16 [2, 2, 2048, 2048], P(None, 'batch', 'seq'), may hold values from -6 to 6
- cotangent: bfloat16 [2, 2, 2048, 2048], P(None, 'batch', 'seq'), may hold values from -6 to 6
- segments: int32 [2, 2, 2048], P(None, 'batch'), may hold values from 0 to 2, as said below
- query_weight: bfloat16 [2048, 2048], P(('batch', 'seq'), 'mp'), may hold values from -0.1875 to 0.1875
- key_weight: bfloat16 [2048, 2048], P(('batch', 'seq'), 'mp'), may hold values from -0.125 to 0.125
- value_weight: bfloat16 [2048, 2048], P(('batch', 'seq'), 'mp'), may hold values from -0.125 to 0.125
- out_weight: bfloat16 [2048, 2048], P('mp', ('batch', 'seq')), may hold values from -2 to 2
- up_weight: bfloat16 [2048, 8192], P(('batch', 'seq'), 'mp'), may hold values from -0.125 to 0.125
- down_weight: bfloat16 [8192, 2048], P('mp', ('batch', 'seq')), may hold values from -0.0625 to 0.0625
- query_bias: float32 [2048], P('mp'), may hold values from -3 to 3
- value_bias: float32 [2048], P('mp'), may hold values from -0.3 to 0.3
- out_bias: float32 [2048], replicated, may hold values from -2 to 2
- up_bias: float32 [8192], P('mp'), may hold values from -3 to 3
- down_bias: float32 [2048], replicated, may hold values from -2 to 2
- attn_gain: float32 [2048], replicated, may hold values from 0.5 to 1.5
- attn_shift: float32 [2048], replicated, may hold values from -2 to 2
- ffn_gain: float32 [2048], replicated, may hold values from 0.5 to 1.5
- ffn_shift: float32 [2048], replicated, may hold values from -2 to 2
Outputs:
- outputs: bfloat16 [2, 2, 2048, 2048], P(None, 'batch', 'seq')
- input_grad: bfloat16 [2, 2, 2048, 2048], P(None, 'batch', 'seq')
- query_weight_grad: float32 [2048, 2048], P(('batch', 'seq'), 'mp')
- key_weight_grad: float32 [2048, 2048], P(('batch', 'seq'), 'mp')
- value_weight_grad: float32 [2048, 2048], P(('batch', 'seq'), 'mp')
- out_weight_grad: float32 [2048, 2048], P('mp', ('batch', 'seq'))
- up_weight_grad: float32 [2048, 8192], P(('batch', 'seq'), 'mp')
- down_weight_grad: float32 [8192, 2048], P('mp', ('batch', 'seq'))
- query_bias_grad: float32 [2048], P('mp')
- value_bias_grad: float32 [2048], P('mp')
- out_bias_grad: float32 [2048], replicated
- up_bias_grad: float32 [8192], P('mp')
- down_bias_grad: float32 [2048], replicated
- attn_gain_grad: float32 [2048], replicated
- attn_shift_grad: float32 [2048], replicated
- ffn_gain_grad: float32 [2048], replicated
- ffn_shift_grad: float32 [2048], replicated
The draws below stay inside these ranges and needn't reach their ends.
Inputs may be any that keep to these rules, and one draw needn't show every extreme that they name: `segments`: each pack holds three documents, numbered 0, 1, 2 in order; the first ends within the pack's first 256 tokens and the last begins within its last 256 tokens, both ends drawn afresh for each pack.
All inputs are finite; a program needn't handle non-finite values.
Results may differ from the reference program's by a relative error of at most 0.029.
Values may be sent and summed in bfloat16 or wider, within the bound.
No kernel may reach another device: no remote copies, remote signals or barrier semaphores. Data moves between devices by JAX's collectives and lax.ppermute only.
A program may use at most 256 MiB of HBM per device.

```python
import jax
import jax.numpy as jnp
from jax import lax

D = 2048
NH = 16
HD = 128
FF = 8192
WINDOW = 1024
MICRO = 2
LENGTH = 2048
TOK_LOC = 256
PACKS = 2


def draw_segments(key, part):
    key = jax.random.fold_in(key, 11)
    first_key, last_key = jax.random.split(key)
    first_end = jax.random.randint(first_key, (MICRO, PACKS, 1), 1, TOK_LOC)
    last_start = LENGTH - jax.random.randint(last_key, (MICRO, PACKS, 1), 1, TOK_LOC)
    places = jnp.arange(LENGTH, dtype=jnp.int32)[None, None, :]
    return (places >= first_end).astype(jnp.int32) + (places >= last_start).astype(jnp.int32)


def steps_of(key, shape, shards, smallest, top_value):
    def one(dim, shards_of):
        heights = jax.random.uniform(jax.random.fold_in(jax.random.fold_in(key, 6), dim), (shards_of,), jnp.float32, smallest / len(shards), top_value / len(shards))
        return jnp.repeat(jnp.exp(heights), shape[dim] // shards_of).reshape((-1,) + (1,) * (len(shape) - dim - 1))

    gain = one(*shards[0])
    for cut in shards[1:]:
        gain = gain * one(*cut)
    return gain


def noise(rng, extent, scale, limit, shards=(), held_as=jnp.bfloat16):
    array = scale * jax.random.normal(rng, extent, jnp.float32)
    if shards:
        array = array * steps_of(rng, extent, shards, -0.22, 0.18)
    return jnp.clip(array, -limit, limit).astype(held_as)


def setup_inputs(seed: int = 0) -> dict:
    splits = jax.random.split(jax.random.key(seed), 19)
    inputs = noise(splits[0], (MICRO, PACKS, LENGTH, D), 1.0, 6.0, ((1, 2), (2, 8)))
    cotangent = noise(splits[1], (MICRO, PACKS, LENGTH, D), 1.0, 6.0, ((1, 2), (2, 8)))
    segments = draw_segments(jax.random.fold_in(splits[18], 71), 0)
    query_weight = noise(splits[3], (D, D), (D // 2) ** -0.5, 0.1875, ((0, 16), (1, 8)))
    key_weight = noise(splits[4], (D, D), D ** -0.5, 0.125, ((0, 16), (1, 8)))
    value_weight = noise(splits[5], (D, D), D ** -0.5, 0.125, ((0, 16), (1, 8)))
    out_weight = noise(splits[6], (D, D), (max(1, D // 256)) ** -0.5, 2.0, ((0, 8), (1, 16)))
    up_weight = noise(splits[7], (D, FF), D ** -0.5, 0.125, ((0, 16), (1, 8)))
    down_weight = noise(splits[8], (FF, D), FF ** -0.5, 0.0625, ((0, 8), (1, 16)))
    query_bias = noise(splits[9], (D,), 0.5, 3.0, ((0, 8),), jnp.float32)
    value_bias = noise(splits[10], (D,), 0.05, 0.3, ((0, 8),), jnp.float32)
    out_bias = noise(splits[11], (D,), 0.3, 2.0, (), jnp.float32)
    up_bias = noise(splits[12], (FF,), 0.5, 3.0, ((0, 8),), jnp.float32)
    down_bias = noise(splits[13], (D,), 0.3, 2.0, (), jnp.float32)
    attn_gain = jnp.clip(jax.random.uniform(splits[14], (D,), jnp.float32, 0.5, 1.5), 0.5, 1.5)
    attn_shift = noise(splits[15], (D,), 0.3, 2.0, (), jnp.float32)
    ffn_gain = jnp.clip(jax.random.uniform(splits[16], (D,), jnp.float32, 0.5, 1.5), 0.5, 1.5)
    ffn_shift = noise(splits[17], (D,), 0.3, 2.0, (), jnp.float32)
    return dict(inputs=inputs, cotangent=cotangent, segments=segments, query_weight=query_weight, key_weight=key_weight, value_weight=value_weight, out_weight=out_weight, up_weight=up_weight, down_weight=down_weight, query_bias=query_bias, value_bias=value_bias, out_bias=out_bias, up_bias=up_bias, down_bias=down_bias, attn_gain=attn_gain, attn_shift=attn_shift, ffn_gain=ffn_gain, ffn_shift=ffn_shift)


NORM_EPSILON = 1e-05
BLOCKED = -1e+30

@jax.custom_vjp
def low(v):
    return lax.optimization_barrier(v.astype(jnp.bfloat16)).astype(jnp.float32)

@jax.custom_vjp
def low_back(v):
    return v

def low_keep(v):
    return (low(v), None)

def low_pass(kept, grad):
    return (grad,)

def back_keep(v):
    return (v, None)

def back_low(kept, grad):
    return (low(grad),)
low.defvjp(low_keep, low_pass)
low_back.defvjp(back_keep, back_low)

def product(left_side, right_side):
    return jnp.dot(left_side, right_side, precision=lax.Precision.HIGHEST)

def norm_rows(values, gain_row, shift_row):
    center = lax.optimization_barrier(jnp.mean(values, axis=-1, keepdims=True))
    centered = values - center
    spread = lax.optimization_barrier(jnp.mean(centered * centered, axis=-1, keepdims=True))
    return centered * lax.rsqrt(spread + NORM_EPSILON) * gain_row + shift_row

def attend(queries, key_rows, value_rows, allowed):

    def one_head(group):
        head_query, head_keys, head_values = group
        scores = low_back(product(head_query, head_keys.T) * HD ** (-0.5))
        scores = jnp.where(allowed, scores, BLOCKED)
        row_max = lax.optimization_barrier(jnp.max(scores, axis=-1, keepdims=True))
        exp_scores = jnp.exp(scores - row_max)
        weights = exp_scores / lax.optimization_barrier(jnp.sum(exp_scores, axis=-1, keepdims=True))
        return product(low(weights), head_values)

    def split_heads(matrix):
        return matrix.reshape(LENGTH, NH, HD).transpose(1, 0, 2)
    attended = lax.map(jax.checkpoint(one_head), (split_heads(queries), split_heads(key_rows), split_heads(value_rows)))
    return attended.transpose(1, 0, 2).reshape(LENGTH, D)

def layer(stream, params, allowed):
    query_weight, key_weight, value_weight, out_weight, up_weight, down_weight, query_bias, value_bias, out_bias, up_bias, down_bias, attn_gain, attn_shift, ffn_gain, ffn_shift = params
    stream_low = low(stream)
    queries = low(low_back(product(stream_low, query_weight) + query_bias))
    key_rows = low(low_back(product(stream_low, key_weight)))
    value_rows = low(low_back(product(stream_low, value_weight) + value_bias))
    attended = low(low_back(attend(queries, key_rows, value_rows, allowed)))
    branch = low_back(product(attended, out_weight) + out_bias)
    first_norm = norm_rows(stream + branch, attn_gain, attn_shift)
    first_low = low(first_norm)
    up_values = low_back(product(first_low, up_weight) + up_bias)
    active = low(jax.nn.gelu(up_values, approximate=True))
    second = low_back(product(active, down_weight) + down_bias)
    return norm_rows(first_norm + second, ffn_gain, ffn_shift)

def forward(stream, params, pack_segs):
    places = jnp.arange(LENGTH, dtype=jnp.int32)
    same_doc = pack_segs[:, None] == pack_segs[None, :]
    near_keys = jnp.abs(places[:, None] - places[None, :]) <= WINDOW // 2
    middle = layer(stream, params, same_doc & near_keys)
    return layer(middle, params, same_doc)

def reference(inputs, cotangent, segments, query_weight, key_weight, value_weight, out_weight, up_weight, down_weight, query_bias, value_bias, out_bias, up_bias, down_bias, attn_gain, attn_shift, ffn_gain, ffn_shift):
    params = tuple((param.astype(jnp.float32) for param in (query_weight, key_weight, value_weight, out_weight, up_weight, down_weight, query_bias, value_bias, out_bias, up_bias, down_bias, attn_gain, attn_shift, ffn_gain, ffn_shift)))
    pack_count = MICRO * PACKS
    streams = inputs.reshape(pack_count, LENGTH, D).astype(jnp.float32)
    upstreams = cotangent.reshape(pack_count, LENGTH, D).astype(jnp.float32)
    pack_rows = segments.reshape(pack_count, LENGTH).astype(jnp.int32)

    def pack_step(totals, pack_item):
        stream, upstream, pack_segs = pack_item

        def run_pack(values, weights):
            return forward(values, weights, pack_segs)
        result, pull_back = jax.vjp(run_pack, stream, params)
        grad_stream, grad_params = pull_back(upstream)
        new_totals = tuple((total_part + new_part for total_part, new_part in zip(totals, grad_params)))
        return (new_totals, (result.astype(jnp.bfloat16), grad_stream.astype(jnp.bfloat16)))
    zero_sums = tuple((jnp.zeros(param.shape, jnp.float32) for param in params))
    totals, (packed_outs, packed_grads) = lax.scan(pack_step, zero_sums, (streams, upstreams, pack_rows))
    shape_full = (MICRO, PACKS, LENGTH, D)
    return (packed_outs.reshape(shape_full), packed_grads.reshape(shape_full), totals[0], totals[1], totals[2], totals[3], totals[4], totals[5], totals[6], totals[7], totals[8], totals[9], totals[10], totals[11], totals[12], totals[13], totals[14])
```

```python
import functools

import jax
import jax.numpy as jnp
from jax import lax
from jax.experimental import pallas as pl
from jax.experimental.pallas import tpu as pltpu
from jax.sharding import Mesh, PartitionSpec as P

AXES = ("core", "ylo", "x", "yhi", "z")
Y = ("ylo", "yhi")
D = 2048
HD = 128
TOK = 256
OWN = 64
REACH = 512
LOW = jnp.bfloat16
F32 = jnp.float32
BLOCKED = -1e30
SCALE = HD ** (-0.5)
LOG2E = 1.4426950408889634
EPSILON = 1e-05
CURVE = 0.7978845608028654
CUBIC = 0.044715


def limit(mib):
    return pltpu.CompilerParams(vmem_limit_bytes=mib * 2**20)


def shape(dims, dtype=LOW):
    return jax.ShapeDtypeStruct(dims, dtype)


def whole(dims):
    return pl.BlockSpec(dims, lambda *_: (0,) * len(dims))


def dot_t(a, b, ca=1, cb=0):
    return lax.dot_general(a, b, (((ca,), (cb,)), ((), ())), preferred_element_type=F32)


def pack_heads_body(q, k, v, o, out):
    for j in range(2):
        at = slice(128 * j, 128 * j + 128)
        for t, part in enumerate((q, k, v)):
            out[:, 384 * j + 128 * t : 384 * j + 128 * t + 128] = part[:, at]
    out[:, 768:] = o[...].T


def pair_heads_body(own, far, out):
    for j in range(2):
        for h, part in enumerate((own, far)):
            slot = 2 * j + h
            out[:, 384 * slot : 384 * slot + 384] = part[:, 384 * j : 384 * j + 384]
            out[:, 1536 + 128 * slot : 1664 + 128 * slot] = part[:, 768 + 128 * j : 896 + 128 * j]


def turn_body(down, out):
    out[...] = down[...].T


def pair_body(own, far, out):
    n = own.shape[1]
    out[:, :n] = own[...]
    out[:, n:] = far[...]


def pack(body, width, *parts):
    return pl.pallas_call(
        body,
        out_shape=shape((128, width)),
        cost_estimate=pl.CostEstimate(flops=0, bytes_accessed=512 * width, transcendentals=0),
        name="pack",
    )(*parts)


def settle_body(spot, p0, p1, p2, p3, out):
    for d, part in enumerate((p0, p1, p2, p3)):
        at = pl.ds(pl.multiple_of((d ^ spot[3]) * OWN, OWN), OWN)
        if len(out.shape) == 2:
            out[at] = part[...]
        else:
            out[:, at] = part[...]


def settle(spot, parts):
    dims = parts[0].shape[:-2] + (TOK, D)
    return pl.pallas_call(
        settle_body,
        in_specs=[pl.BlockSpec(memory_space=pltpu.SMEM)] + [pl.BlockSpec(memory_space=pltpu.VMEM)] * 4,
        out_specs=pl.BlockSpec(memory_space=pltpu.VMEM),
        out_shape=shape(dims),
        cost_estimate=pl.CostEstimate(flops=0, bytes_accessed=2**22, transcendentals=0),
        name="settle",
    )(spot, *parts)


def rows_body(kind, spot, p0, p1, p2, p3, w, *refs):
    step = pl.program_id(0)
    kept = pl.multiple_of(spot[1] * (D // 2), D // 2)
    sent = pl.multiple_of((1 - spot[1]) * (D // 2), D // 2)
    extra = refs[0] if kind in ("qkv", "up", "slope") else None
    keep, send = refs[1:3] if extra is not None else refs[:2]
    outs = refs[3:] if extra is not None else refs[2:]

    @pl.when(step == 0)
    def _():
        for i, p in enumerate((p0, p1, p2, p3)):
            keep[OWN * i : OWN * i + OWN] = p[:, pl.ds(kept, D // 2)]
            send[OWN * i : OWN * i + OWN] = p[:, pl.ds(sent, D // 2)]

    values = dot_t(keep[...], w[pl.ds(kept, D // 2)]) + dot_t(send[...], w[pl.ds(sent, D // 2)])
    if kind == "qkv":
        values = values + extra[...]
    if kind in ("qkv", "heads"):
        low = values.astype(LOW)
        for d in range(4):

            @pl.when(step == d)
            def _():
                outs[d][...] = low
    elif kind == "up":
        values = values + extra[...]
        square = values * values
        bend = jnp.tanh(CURVE * (values + CUBIC * (square * values)))
        outs[0][...] = (0.5 * values * (1.0 + bend)).astype(LOW)
        slope = 0.5 * (1.0 + bend) + 0.5 * values * (1.0 - bend * bend) * (CURVE * (1.0 + 3.0 * CUBIC * square))
        outs[1][...] = slope.astype(LOW)
    else:
        low = (values * extra[...].astype(F32)).astype(LOW)
        outs[0][...] = low
        outs[1][...] = jnp.sum(low.astype(F32), axis=0, keepdims=True)


def rows_mm(kind, spot, pieces, weight, n, first, extra=None):
    tile = n // 4
    by_slot = kind in ("qkv", "heads")

    def column(i, spot):
        return (0, i ^ spot[0]) if by_slot else (0, i)

    def weight_column(i, spot):
        return (0, first // tile + column(i, spot)[1])

    in_specs = [whole((OWN, D))] * 4 + [pl.BlockSpec((D, tile), weight_column)]
    args = list(pieces) + [weight]
    if extra is not None:
        in_specs.append(pl.BlockSpec((extra.shape[0], tile), column))
        args.append(extra)
    half = shape((TOK, D // 2))
    if by_slot:
        outs = [half, half] + [shape((TOK, tile))] * 4
        out_specs = [whole((TOK, D // 2))] * 2 + [whole((TOK, tile))] * 4
    else:
        outs = [half, half, shape((TOK, n)), shape((TOK, n)) if kind == "up" else shape((1, n), F32)]
        block = pl.BlockSpec((TOK, tile), column)
        out_specs = [whole((TOK, D // 2))] * 2 + [block, block if kind == "up" else pl.BlockSpec((1, tile), column)]
    return pl.pallas_call(
        functools.partial(rows_body, kind),
        grid_spec=pltpu.PrefetchScalarGridSpec(num_scalar_prefetch=1, grid=(4,), in_specs=in_specs, out_specs=out_specs),
        out_shape=outs,
        compiler_params=limit(28),
        cost_estimate=pl.CostEstimate(flops=2 * TOK * D * n, bytes_accessed=2 * D * n + 8 * TOK * D, transcendentals=TOK * n),
        name="rows_" + kind,
    )(spot, *args)


def split_rows(values, outs, to):
    outs[0][:, to] = values[:OWN]
    for i in range(1, 4):
        outs[i][:, to] = values[OWN * i : OWN * i + OWN].astype(LOW)


def scatter_body(n_parts, spot, *refs):
    parts, w = refs[:n_parts], refs[n_parts]
    outs = refs[n_parts + 1 : n_parts + 5]
    if n_parts == 1:
        rows = parts[0]
    else:
        rows, sums = refs[n_parts + 5], refs[n_parts + 6]

        @pl.when(pl.program_id(0) == 0)
        def _():
            width = parts[0].shape[1]
            for d, part in enumerate(parts):
                at = pl.ds(pl.multiple_of((d ^ spot[0]) * width, 128), width)
                rows[:, at] = part[...]
                sums[:, at] = jnp.sum(part[...].astype(F32), axis=0, keepdims=True)

    split_rows(dot_t(rows[...], w[...], 1, 1), outs, slice(None))


def scatter_mm(spot, parts, weight, k, first):
    tile = 512
    in_specs = [whole(p.shape) for p in parts] + [pl.BlockSpec((tile, k), lambda i, spot: (i, first // k))]
    block = pl.BlockSpec((OWN, tile), lambda i, spot: (0, i))
    outs = [shape((OWN, D), F32)] + [shape((OWN, D))] * 3
    out_specs = [block] * 4
    if len(parts) > 1:
        outs += [shape((TOK, k)), shape((1, k), F32)]
        out_specs += [whole((TOK, k)), whole((1, k))]
    return pl.pallas_call(
        functools.partial(scatter_body, len(parts)),
        grid_spec=pltpu.PrefetchScalarGridSpec(
            num_scalar_prefetch=1, grid=(D // tile,), in_specs=in_specs, out_specs=out_specs
        ),
        out_shape=outs,
        compiler_params=limit(28),
        cost_estimate=pl.CostEstimate(flops=2 * TOK * D * k, bytes_accessed=2 * D * k + 4 * TOK * D, transcendentals=0),
        name="scatter_mm",
    )(spot, *parts, weight)


def term_body(groups, *refs):
    lefts = [refs[8 * g : 8 * g + 4] for g in range(groups)]
    rights = [refs[8 * g + 4 : 8 * g + 8] for g in range(groups)]
    out, turned = refs[8 * groups], refs[8 * groups + 1 :]
    step = pl.program_id(0)

    @pl.when(step == 0)
    def _():
        for g in range(groups):
            for i in range(4):
                turned[g][:, TOK * i : TOK * i + TOK] = lefts[g][i][...].T

    parts = []
    for g in range(groups):
        total = None
        for i in range(4):
            part = dot_t(turned[g][:, TOK * i : TOK * i + TOK], rights[g][i][...])
            total = part if total is None else total + part
        parts.append(total.astype(LOW))
    if groups == 1:
        out[...] = parts[0]
        return
    widths = [part.shape[1] for part in parts]
    for slot in range(4):

        @pl.when(step == slot)
        def _():
            first = (slot & 1) * 2 * sum(widths)
            for part, width in zip(parts, widths):
                at = first + (slot >> 1) * width
                out[:, at : at + width] = part
                first += 2 * width


def weight_terms(groups):
    widths = [rights[0].shape[1] // 4 for _, rights in groups]
    n = sum(widths)
    in_specs, args = [], []
    for (lefts, rights), width in zip(groups, widths):
        in_specs += [whole((TOK, 1024))] * 4 + [pl.BlockSpec((TOK, width), lambda i: (0, i))] * 4
        args += list(lefts) + list(rights)
    return pl.pallas_call(
        functools.partial(term_body, len(groups)),
        grid=(4,),
        in_specs=in_specs,
        out_specs=pl.BlockSpec((1024, n), lambda i: (0, i)) if len(groups) == 1 else whole((1024, 4 * n)),
        out_shape=shape((1024, 4 * n)),
        scratch_shapes=[pltpu.VMEM((1024, 1024), LOW)] * len(groups),
        compiler_params=limit(32),
        cost_estimate=pl.CostEstimate(flops=8 * 1024 * 1024 * n, bytes_accessed=8 * 1024 * n + 2**23, transcendentals=0),
        name="weight_terms",
    )(*args)


def near(marks, keys, windowed):
    return jnp.abs(marks - keys) <= (REACH if windowed else 2047.0)


def load_heads(pieces, queries, keys, values):
    for i, piece in enumerate(pieces):
        at = slice(TOK * i, TOK * i + TOK)
        if i < 4:
            queries[at] = piece[:, :HD]
        keys[at] = piece[:, HD : 2 * HD]
        values[at] = piece[:, 2 * HD :]


def fwd_body(windowed, *refs):
    pieces, qmark, kmark = refs[:8], refs[8], refs[9]
    outs, lse, queries, keys, values = refs[10:14], *refs[14:]
    step = pl.program_id(0)

    @pl.when(step == 0)
    def _():
        load_heads(pieces, queries, keys, values)

    query = queries[pl.ds(pl.multiple_of(step * TOK, TOK), TOK)]
    s = dot_t(keys[...], query, 1, 1)
    s = jnp.where(near(qmark[...], kmark[...], windowed), s, BLOCKED)
    top = jnp.max(s, axis=0, keepdims=True)
    p = jnp.exp2((s - top) * (SCALE * LOG2E))
    total = jnp.sum(p, axis=0, keepdims=True)
    mixed = (dot_t(values[...], p.astype(LOW), 0, 0) / total).T.astype(LOW)
    for d in range(4):

        @pl.when(step == d)
        def _():
            outs[d][...] = mixed

    lse[...] = top * (SCALE * LOG2E) + jnp.log2(total)


def mark_specs():
    return [pl.BlockSpec((1, TOK), lambda i: (0, i)), whole((8 * TOK, 1))]


def attend_fwd(pieces, mark, windowed):
    n = 4 * TOK
    *mixed, lse = pl.pallas_call(
        functools.partial(fwd_body, windowed),
        grid=(4,),
        in_specs=[whole((TOK, 3 * HD))] * 8 + mark_specs(),
        out_specs=[whole((TOK, HD))] * 4 + [pl.BlockSpec((1, TOK), lambda i: (0, i))],
        out_shape=[shape((TOK, HD))] * 4 + [shape((1, n), F32)],
        scratch_shapes=[pltpu.VMEM((n, HD), LOW), pltpu.VMEM((2 * n, HD), LOW), pltpu.VMEM((2 * n, HD), LOW)],
        compiler_params=limit(24),
        cost_estimate=pl.CostEstimate(flops=8 * n * n * HD, bytes_accessed=2**22, transcendentals=2 * n * n),
        name="attend_fwd",
    )(*pieces, *mark)
    return mixed, lse


def bwd_body(windowed, *refs):
    pieces, grads, outs, lse, qmark, kmark = refs[:8], refs[8:12], refs[12:16], *refs[16:19]
    dq, own, far, queries, keys, values, g_all, o_all, acc = refs[19:23], *refs[23:]
    step = pl.program_id(0)
    n = 4 * TOK

    @pl.when(step == 0)
    def _():
        load_heads(pieces, queries, keys, values)
        for i in range(4):
            g_all[TOK * i : TOK * i + TOK] = grads[i][...]
            o_all[TOK * i : TOK * i + TOK] = outs[i][...]
        acc[...] = jnp.zeros_like(acc)

    at = pl.ds(pl.multiple_of(step * TOK, TOK), TOK)
    query, grad, out = queries[at], g_all[at], o_all[at]
    dots = jnp.sum((grad.astype(F32) * out.astype(F32)).T, axis=0, keepdims=True)
    s = dot_t(keys[...], query, 1, 1)
    s = jnp.where(near(qmark[...], kmark[...], windowed), s, BLOCKED)
    p = jnp.exp2(s * (SCALE * LOG2E) - lse[...])
    ds = (p * (dot_t(values[...], grad, 1, 1) - dots)).astype(LOW)
    acc[:, :HD] += dot_t(ds, query)
    acc[:, HD:] += dot_t(p.astype(LOW), grad)
    turned = (dot_t(keys[...], ds, 0, 0) * SCALE).T.astype(LOW)
    for d in range(4):

        @pl.when(step == d)
        def _():
            dq[d][...] = turned

    @pl.when(step == 3)
    def _():
        for ref, start in ((own, 0), (far, n)):
            ref[:, :HD] = acc[start : start + n, :HD] * SCALE
            ref[:, HD:] = acc[start : start + n, HD:]


def attend_bwd(pieces, grads, mixed, lse, mark, windowed):
    n = 4 * TOK
    *dq, own, far = pl.pallas_call(
        functools.partial(bwd_body, windowed),
        grid=(4,),
        in_specs=[whole((TOK, 3 * HD))] * 8
        + [whole((TOK, HD))] * 8
        + [pl.BlockSpec((1, TOK), lambda i: (0, i))]
        + mark_specs(),
        out_specs=[whole((TOK, HD))] * 4 + [whole((n, 2 * HD))] * 2,
        out_shape=[shape((TOK, HD))] * 4 + [shape((n, 2 * HD), F32)] * 2,
        scratch_shapes=[pltpu.VMEM((n, HD), LOW), pltpu.VMEM((2 * n, HD), LOW), pltpu.VMEM((2 * n, HD), LOW)]
        + [pltpu.VMEM((n, HD), LOW)] * 2
        + [pltpu.VMEM((2 * n, 2 * HD), F32)],
        compiler_params=limit(36),
        cost_estimate=pl.CostEstimate(flops=20 * n * n * HD, bytes_accessed=2**23, transcendentals=2 * n * n),
        name="attend_bwd",
    )(*pieces, *grads, *mixed, lse, *mark)
    return dq, own, far


def join_body(*refs):
    dq, own, far, outs = refs[:4], refs[4], refs[5], refs[6:]
    for d in range(4):
        at = slice(TOK * d, TOK * d + TOK)
        outs[d][:, :HD] = dq[d][...]
        outs[d][:, HD:] = (own[at] + far[at]).astype(LOW)


def join_heads(dq, own, far):
    return pl.pallas_call(
        join_body,
        out_shape=[shape((TOK, 3 * HD))] * 4,
        compiler_params=limit(16),
        cost_estimate=pl.CostEstimate(flops=2**18, bytes_accessed=2**22, transcendentals=0),
        name="join_heads",
    )(*dq, own, far)


def swap(values, axis, bits, size=4):
    if axis == Y:
        bits = (bits & 1) * 2 + (bits >> 1)
    return lax.ppermute(values, axis, [(i, i ^ bits) for i in range(size)])


def sibling(values):
    return swap(values, "core", 1, 2)


def exchange(pieces, axis):
    got = {d: swap(pieces[d], axis, d) for d in (2, 1, 3)}
    return [pieces[0], got[1], got[2], got[3]]


def gather(piece, axis):
    return exchange([piece] * 4, axis)


def four_sum(parts):
    return (parts[0].astype(F32) + parts[2].astype(F32)) + (parts[1].astype(F32) + parts[3].astype(F32))


def tie(*values):
    return lax.optimization_barrier(values)


def pick(stacked, index):
    return lax.dynamic_index_in_dim(stacked, index, 0, keepdims=False)


def norm(values):
    center = jnp.mean(values, axis=-1, keepdims=True)
    centered = values - center
    spread = jnp.mean(centered * centered, axis=-1, keepdims=True)
    scale = lax.rsqrt(spread + EPSILON)
    return centered * scale, scale


def norm_back(grad, normed, scale, gain):
    terms = jnp.sum(grad * normed, axis=0), jnp.sum(grad, axis=0)
    tilted = grad * gain
    back = tilted - jnp.mean(tilted, axis=-1, keepdims=True)
    back = (back - normed * jnp.mean(tilted * normed, axis=-1, keepdims=True)) * scale
    return back, terms


def line_sum(values, axis):
    return four_sum(gather(values, axis))


def layer_forward(spot, stream, pieces, matrices, vectors, mark, windowed):
    heads_matrix, up_matrix, down_matrix = matrices
    qkv_bias, up_bias, out_bias, down_bias, attn_gain, attn_shift, ffn_gain, ffn_shift = vectors
    rows_keep, rows_send, *heads = rows_mm("qkv", spot, pieces, heads_matrix, 1536, 0, qkv_bias)
    heads = exchange(heads, "x")
    heads = heads + [sibling(h) for h in heads]
    mixed, lse = attend_fwd(heads, mark, windowed)
    *branch, attended, _ = scatter_mm(spot, exchange(mixed, "x"), heads_matrix, 512, 1536)
    normed, scale = norm(stream + four_sum(exchange(branch, "z")) + out_bias)
    first = normed * attn_gain + attn_shift
    first_keep, first_send, active, slope = rows_mm("up", spot, gather(first.astype(LOW), "z"), up_matrix, 2048, 0, up_bias)
    second = four_sum(exchange(scatter_mm(spot, [active], down_matrix, 2048, 0), "z"))
    normed_two, scale_two = norm(first + second + down_bias)
    result = normed_two * ffn_gain + ffn_shift
    saved = (heads, mixed, lse, normed, scale, slope, normed_two, scale_two)
    halves = [(rows_keep, sibling(rows_send)), (first_keep, sibling(first_send))]
    units = [(attended, sibling(attended)), (active, sibling(active))]
    return result, saved, halves, units


def layer_backward(spot, grad, saved, halves, units, matrices, vectors, mark, windowed, earlier=None):
    heads_matrix, up_matrix, down_matrix = matrices
    qkv_bias, up_bias, out_bias, down_bias, attn_gain, attn_shift, ffn_gain, ffn_shift = vectors
    heads, mixed, lse, normed, scale, slope, normed_two, scale_two = saved
    last = earlier is not None
    grad_summed, ffn_terms = norm_back(grad, normed_two, scale_two, ffn_gain)
    second_own = grad_summed.astype(LOW)
    second_keep, second_send, grad_up, up_sums = rows_mm("slope", spot, gather(second_own, "z"), down_matrix, 2048, 0, slope)
    down_pair = ((second_keep, sibling(second_send)), units[1])
    up_pair = (halves[1], (grad_up, sibling(grad_up)))
    partial = scatter_mm(spot, [grad_up], up_matrix, 2048, 0)
    if last:
        down_term = weight_terms([join_pairs(down_pair, earlier[3])])
        own_part, down_term = tie(partial[0], down_term)
        partial = [own_part, *partial[1:]]
        down_sum = lax.psum_scatter(down_term, ("ylo", "x"), scatter_dimension=0, tiled=True)
    grad_first = four_sum(exchange(partial, "z")) + grad_summed
    grad_residual, attn_terms = norm_back(grad_first, normed, scale, attn_gain)
    branch_own = grad_residual.astype(LOW)
    if last:
        up_term = weight_terms([join_pairs(up_pair, earlier[2])])
        branch_own, up_term = tie(branch_own, up_term)
        up_sum = lax.psum_scatter(up_term, ("ylo", "x"), scatter_dimension=0, tiled=True)
    branch_keep, branch_send, *grad_heads = rows_mm("heads", spot, gather(branch_own, "z"), heads_matrix, 512, 1536)
    out_pair = ((branch_keep, sibling(branch_send)), units[0])
    grad_queries, own_terms, far_terms = attend_bwd(heads, exchange(grad_heads, "x"), mixed, lse, mark, windowed)
    grad_parts = exchange(join_heads(grad_queries, own_terms, sibling(far_terms)), "x")
    *partial, grad_packed, head_sums = scatter_mm(spot, grad_parts, heads_matrix, 1536, 0)
    qkv_pair = (halves[0], (grad_packed, sibling(grad_packed)))
    own_sums = (
        jnp.sum(branch_own.astype(F32), axis=0),
        jnp.sum(second_own.astype(F32), axis=0),
        attn_terms[0],
        attn_terms[1],
        ffn_terms[0],
        ffn_terms[1],
    )
    sums = (jnp.stack(own_sums), head_sums, up_sums)
    if last:
        rest = weight_terms([join_pairs(qkv_pair, earlier[0]), join_pairs(out_pair, earlier[1])])
        own_part, rest, *sums = tie(partial[0], rest, *sums)
        partial = [own_part, *partial[1:]]
        rest = lax.psum_scatter(rest, ("ylo", "x"), scatter_dimension=0, tiled=True)
    grad_stream = four_sum(exchange(partial, "z")) + grad_residual
    if not last:
        return grad_stream, (qkv_pair, out_pair, up_pair, down_pair), sums
    return grad_stream, [add_far(total) for total in (rest, up_sum, down_sum)], sums


def add_far(total):
    n = total.shape[1] // 2
    return total[:, :n].astype(F32) + swap(total[:, n:], "yhi", 1, 2).astype(F32)


def join_pairs(one, two):
    return list(one[0]) + list(two[0]), list(one[1]) + list(two[1])


TURN = [(0, 0), (1, 2), (2, 1), (3, 3)]


def turn_same(values):
    return lax.ppermute(values, ("core", "ylo"), TURN)


def turn_other(values):
    perm = [(c * 4 + l * 2 + h, l * 4 + c * 2 + 1 - h) for c in range(2) for l in range(2) for h in range(2)]
    return lax.ppermute(values, ("core", "ylo", "yhi"), perm)


def by_micro(yhi, same, other):
    return jnp.stack([jnp.where(yhi == 0, same, other), jnp.where(yhi == 0, other, same)])


def absolute_yhi(values, yhi):
    return jnp.where(yhi == 0, values, values[::-1])


def deliver_z_first(yhi, spot, own):
    rows = settle(spot, gather(own, "z"))
    return by_micro(yhi, turn_same(rows), turn_other(rows))[:, None]


def deliver_y_first(yhi, spot, own):
    both = by_micro(yhi, turn_same(own), turn_other(own))
    return settle(spot, gather(both, "z"))[:, None]


def shards(
    inputs,
    cotangent,
    segments,
    query_weight,
    key_weight,
    value_weight,
    out_weight,
    up_weight,
    down_weight,
    query_bias,
    value_bias,
    out_bias,
    up_bias,
    down_bias,
    attn_gain,
    attn_shift,
    ffn_gain,
    ffn_shift,
):
    core, ylo, x, yhi, z = (lax.axis_index(name) for name in AXES)
    spot = jnp.stack([x, core, ylo, z]).astype(jnp.int32)
    local = pack(pack_heads_body, 1024, query_weight, key_weight, value_weight, out_weight)
    local = pack(pair_heads_body, 2048, local, swap(local, "yhi", 1, 2))
    own_rows = pick(pick(inputs, yhi)[0].reshape(4, OWN, D), z)
    own_rows, local = tie(own_rows, local)
    heads_matrix = lax.all_gather(local, ("core", "ylo", "x"), axis=0, tiled=True)
    own_rows = turn_same(own_rows)
    pieces = gather(own_rows, "z")
    *pieces, up_weight, down_weight = tie(*pieces, up_weight, down_weight)
    hidden_matrices = []
    for own in (up_weight, pack(turn_body, 1024, down_weight)):
        local = pack(pair_body, 2048, own, swap(own, "yhi", 1, 2))
        hidden_matrices.append(lax.all_gather(local, ("core", "ylo", "x"), axis=0, tiled=True))
    matrices = (heads_matrix, *hidden_matrices)
    bias_own = jnp.concatenate([query_bias, value_bias, up_bias])
    bias = (bias_own, swap(bias_own, "yhi", 1, 2))
    none = jnp.zeros((128,), F32)
    qkv_bias = jnp.concatenate(
        [
            part
            for j in range(2)
            for h in range(2)
            for part in (bias[h][128 * j : 128 * j + 128], none, bias[h][256 + 128 * j : 384 + 128 * j])
        ]
    )
    up_all = jnp.concatenate([bias[h][512:] for h in range(2)])
    vectors = (qkv_bias[None], up_all[None], out_bias, down_bias, attn_gain, attn_shift, ffn_gain, ffn_shift)
    top_grad = turn_same(pick(pick(cotangent, yhi)[0].reshape(4, OWN, D), z)).astype(F32)
    seg_here = pick(segments, yhi)[0].astype(F32)
    seg_pack = jnp.where(core == ylo, seg_here, sibling(seg_here)).astype(jnp.int32).reshape(2, 4, 4, 64)
    x_order = x ^ jnp.arange(4, dtype=jnp.int32)
    z_order = z ^ jnp.arange(4, dtype=jnp.int32)

    def seg_of(core):
        mine = pick(seg_pack, core)
        mine = jnp.concatenate([pick(mine, x_order[i])[None] for i in range(4)], axis=0)
        return jnp.concatenate([lax.dynamic_slice_in_dim(mine, z_order[i], 1, 1) for i in range(4)], axis=1).reshape(-1)

    def places(core):
        first = (core * 4 + x_order)[:, None, None] * 256 + z_order[None, :, None] * 64
        return (first + jnp.arange(64, dtype=jnp.int32)[None, None, :]).reshape(-1)

    mark = jnp.concatenate([8192 * seg_of(who) + places(who) for who in (core, 1 - core)]).astype(F32)
    mark = (mark[None, :1024], mark[:, None])
    stream = own_rows.astype(F32)
    middle, saved_one, halves_one, units_one = layer_forward(spot, stream, pieces, matrices, vectors, mark, True)
    pieces = gather(middle.astype(LOW), "z")
    final, saved_two, halves_two, units_two = layer_forward(spot, middle, pieces, matrices, vectors, mark, False)
    outputs = deliver_z_first(yhi, spot, final.astype(LOW))
    grad, pairs, sums_two = layer_backward(
        spot, top_grad, saved_two, halves_two, units_two, matrices, vectors, mark, False
    )
    grad, outputs = tie(grad, outputs)
    grad, scattered, sums_one = layer_backward(
        spot, grad, saved_one, halves_one, units_one, matrices, vectors, mark, True, pairs
    )
    input_grad = deliver_y_first(yhi, spot, grad.astype(LOW))
    rest, up_weight_grad, down_turned = scattered
    query_grad, key_grad, value_grad = (
        jnp.concatenate([rest[:, 384 * j + 128 * t : 384 * j + 128 * t + 128] for j in range(2)], axis=1) for t in range(3)
    )
    out_weight_grad = rest[:, 768:].T
    down_weight_grad = down_turned.T
    own_sums, head_sums, hidden_sums = (one + two for one, two in zip(sums_one, sums_two))
    own_sums = line_sum(own_sums, "z").reshape(-1, 128)
    head_sums = jnp.stack([absolute_yhi(head_sums.reshape(2, 2, 3, 128)[j], yhi) for j in range(2)])
    hidden_sums = absolute_yhi(hidden_sums.reshape(2, 1024), yhi)
    sums = jnp.concatenate([own_sums, head_sums.reshape(-1, 128), hidden_sums.reshape(-1, 128)])
    sums = line_sum(line_sum(sums + sibling(sums), "x"), Y).reshape(-1)
    own = sums[: 6 * D].reshape(6, D)
    heads = sums[6 * D : 6 * D + 1536].reshape(2, 2, 3, 128)
    heads = lax.dynamic_index_in_dim(heads, yhi, 1, keepdims=False)
    hidden_all = pick(sums[6 * D + 1536 :].reshape(2, 1024), yhi)
    return (
        outputs,
        input_grad,
        query_grad,
        key_grad,
        value_grad,
        out_weight_grad,
        up_weight_grad,
        down_weight_grad,
        heads[:, 0].reshape(-1),
        heads[:, 2].reshape(-1),
        own[0],
        hidden_all,
        own[1],
        own[2],
        own[3],
        own[4],
        own[5],
    )


def solution(mesh):
    split = Mesh(mesh.devices.reshape(2, 2, 4, 2, 4), AXES)
    token = P(None, "core", ("ylo", "x"), None)
    inner = P(("core", "ylo", "x"), ("yhi", "z"))
    outer = P(("yhi", "z"), ("core", "ylo", "x"))
    unit = P(("yhi", "z"))
    matrix = (inner, inner, inner, outer, inner, outer)
    vector = (unit, unit, P(), unit, P(), P(), P(), P(), P())
    in_specs = (token, token, P(None, "core", None)) + matrix + vector
    out_specs = (token, token) + matrix + vector
    return jax.shard_map(shards, mesh=split, in_specs=in_specs, out_specs=out_specs, check_vma=False)
```

```python
import functools

import jax
import jax.numpy as jnp
from jax import lax
from jax.experimental import pallas as pl
from jax.experimental.pallas import tpu as pltpu
from jax.sharding import Mesh, PartitionSpec as P

AXES = ("core", "ylo", "x", "yhi", "z")
Y = ("ylo", "yhi")
ROWS = ("core", "ylo", "x")
D = 2048
HD = 128
TOK = 256
OWN = 64
REACH = 512
LOW = jnp.bfloat16
F32 = jnp.float32
BLOCKED = -1e30
SCALE = HD ** (-0.5)
LOG2E = 1.4426950408889634
EPSILON = 1e-05
CURVE = 0.7978845608028654
CUBIC = 0.044715


def shape(dims, dtype=LOW):
    return jax.ShapeDtypeStruct(dims, dtype)


def dot_t(a, b, ca=1, cb=0):
    return lax.dot_general(a, b, (((ca,), (cb,)), ((), ())), preferred_element_type=F32)


def call(name, body, outs, *args, spot=None, scratch=(), mib=12, flops=0, size=2**21, exps=0):
    specs = [pl.BlockSpec(memory_space=pltpu.VMEM)] * len(args)
    if spot is not None:
        args = (spot,) + args
        specs = [pl.BlockSpec(memory_space=pltpu.SMEM)] + specs
    return pl.pallas_call(
        body,
        in_specs=specs,
        out_specs=[pl.BlockSpec(memory_space=pltpu.VMEM)] * len(outs),
        out_shape=outs,
        scratch_shapes=scratch,
        compiler_params=pltpu.CompilerParams(vmem_limit_bytes=mib * 2**20),
        cost_estimate=pl.CostEstimate(flops=flops, bytes_accessed=size, transcendentals=exps),
        name=name,
    )(*args)


def at_block(index, size):
    return pl.ds(pl.multiple_of(index * size, size), size)


def pack_heads_body(q, k, v, o, out):
    for j in range(2):
        at = slice(128 * j, 128 * j + 128)
        for t, part in enumerate((q, k, v)):
            out[:, 384 * j + 128 * t : 384 * j + 128 * t + 128] = part[:, at]
    out[:, 768:] = o[...].T


def turn_body(down, out):
    out[...] = down[...].T


def join_heads_columns(own, far, out, rows):
    for j in range(2):
        for h, part in enumerate((own, far)):
            slot = 2 * j + h
            out[rows, 384 * slot : 384 * slot + 384] = part[:, 384 * j : 384 * j + 384]
            out[rows, 1536 + 128 * slot : 1664 + 128 * slot] = part[:, 768 + 128 * j : 896 + 128 * j]


def pair_body(heads, spot, *refs):
    parts, out = refs[:-1], refs[-1]
    for ylo in range(2):
        rows = at_block(ylo ^ spot[2], 128)
        if heads:
            join_heads_columns(parts[ylo], parts[ylo + 2], out, rows)
            continue
        for i, d in enumerate((ylo, ylo + 2, ylo + 4, ylo + 6)):
            out[rows, 1024 * i : 1024 * i + 1024] = parts[d][...]


def pair(heads, spot, parts):
    outs = [shape((256, 2048 if heads else 4096))]
    return call("pair", functools.partial(pair_body, heads), outs, *parts, spot=spot)[0]


def pack(body, width, *parts):
    return call("pack", body, [shape((128, width))], *parts)[0]


def load_body(first, source, kept, sems):
    copies = []
    for core in range(2):
        for ylo in range(2):
            for x in range(4):
                at, to = 256 * (4 * core + x) + 128 * ylo, 1024 * core + 512 * ylo + 128 * x
                part = source.at[pl.ds(at, 128), pl.ds(first, 2048)]
                copies.append(pltpu.make_async_copy(part, kept.at[pl.ds(to, 128)], sems.at[len(copies)]))
    for copy in copies:
        copy.start()
    for copy in copies:
        copy.wait()


def load(matrix, first=0):
    return pl.pallas_call(
        functools.partial(load_body, first),
        in_specs=[pl.BlockSpec(memory_space=pl.ANY)],
        out_specs=pl.BlockSpec(memory_space=pltpu.VMEM),
        out_shape=pltpu.VMEM((D, 2048), LOW),
        scratch_shapes=[pltpu.SemaphoreType.DMA((16,))],
        compiler_params=pltpu.CompilerParams(vmem_limit_bytes=2**22),
        cost_estimate=pl.CostEstimate(flops=0, bytes_accessed=4 * matrix.size, transcendentals=0),
        name="load",
    )(pltpu.with_memory_space_constraint(matrix, pltpu.HBM))


def held(matrix):
    return pltpu.with_memory_space_constraint(matrix, pltpu.VMEM)


def settle_body(spot, p0, p1, p2, p3, out):
    for d, part in enumerate((p0, p1, p2, p3)):
        at = at_block(d ^ spot[3], OWN)
        if len(out.shape) == 2:
            out[at] = part[...]
        else:
            out[:, at] = part[...]


def settle(spot, parts):
    return call("settle", settle_body, [shape(parts[0].shape[:-2] + (TOK, D))], *parts, spot=spot)[0]


def four(refs, at):
    p = [ref[at].astype(F32) for ref in refs]
    return (p[0] + p[2]) + (p[1] + p[3])


def rows_body(kind, first, spot, p0, p1, p2, p3, w, *refs):
    extra = refs[0] if kind != "heads" else None
    keep, send, *outs = refs[1:] if kind != "heads" else refs
    kept, sent = at_block(spot[1], D // 2), at_block(1 - spot[1], D // 2)
    for i, p in enumerate((p0, p1, p2, p3)):
        keep[OWN * i : OWN * i + OWN] = p[:OWN, kept]
        send[OWN * i : OWN * i + OWN] = p[:OWN, sent]
    if p0.shape[0] > OWN:
        *outs, sums = outs
        sums[...] = four((p0, p1, p2, p3), slice(OWN, OWN + 16))

    def product(at):
        return dot_t(keep[...], w[kept, at]) + dot_t(send[...], w[sent, at])

    if kind in ("qkv", "heads"):
        width = outs[0].shape[1]
        for d in range(4):
            slot = d ^ spot[0]
            values = product(pl.ds(pl.multiple_of(first + slot * width, 128), width))
            if kind == "qkv":
                values = values + extra[:, at_block(slot, width)]
            outs[d][...] = values.astype(LOW)
        return
    tile = 512
    for i in range(4):
        at = slice(tile * i, tile * i + tile)
        values = product(at)
        if kind == "up":
            values = values + extra[:, at]
            square = values * values
            bend = jnp.tanh(CURVE * (values + CUBIC * (square * values)))
            outs[0][:, at] = (0.5 * values * (1.0 + bend)).astype(LOW)
            slope = 0.5 * (1.0 + bend) + 0.5 * values * (1.0 - bend * bend) * (CURVE * (1.0 + 3.0 * CUBIC * square))
            outs[1][:, at] = slope.astype(LOW)
        else:
            low = (values * extra[:, at].astype(F32)).astype(LOW)
            outs[0][:, at] = low
            outs[1][:, at] = jnp.sum(low.astype(F32), axis=0, keepdims=True)


def rows_mm(kind, spot, pieces, weight, extra=None):
    half = shape((TOK, D // 2))
    n, first, outs = {
        "qkv": (1536, 0, [shape((TOK, 384))] * 4),
        "heads": (512, 1536, [shape((TOK, HD))] * 4),
        "up": (2048, 0, [shape((TOK, 2048))] * 2),
        "slope": (2048, 0, [shape((TOK, 2048)), shape((1, 2048), F32)]),
    }[kind]
    args = (held(weight),) if extra is None else (held(weight), extra)
    if pieces[0].shape[0] > OWN:
        outs = [*outs, shape((16, D), F32)]
    return call(
        "rows_" + kind,
        functools.partial(rows_body, kind, first),
        [half, half, *outs],
        *pieces,
        *args,
        spot=spot,
        mib=12,
        flops=2 * TOK * D * n,
        size=2 * D * n,
        exps=TOK * n if kind == "up" else 0,
    )


def scatter_body(n_parts, first, k, spot, *refs):
    parts, w, outs = refs[:n_parts], refs[n_parts], refs[n_parts + 1 : n_parts + 5]
    if n_parts == 1:
        rows = parts[0]
    else:
        rows = refs[n_parts + 5]
        for d, part in enumerate(parts):
            rows[:, at_block(d ^ spot[0], k // 4)] = part[...]
    tile = 512
    for i in range(D // tile):
        to = slice(tile * i, tile * i + tile)
        values = dot_t(rows[...], w[to, first : first + k], 1, 1)
        outs[0][:, to] = values[:OWN]
        for d in range(1, 4):
            outs[d][:, to] = values[OWN * d : OWN * d + OWN].astype(LOW)


def scatter_mm(spot, parts, weight, k, first):
    outs = [shape((OWN, D), F32)] + [shape((OWN, D))] * 3
    if len(parts) > 1:
        outs.append(shape((TOK, k)))
    return call(
        "scatter_mm",
        functools.partial(scatter_body, len(parts), first, k),
        outs,
        *parts,
        held(weight),
        spot=spot,
        flops=2 * TOK * D * k,
        size=2 * D * k,
    )


def fetched(refs, olds, buffers, sems, chunks):
    ready, copies, at = [], [], 0
    for ref, old, count in zip(refs, olds, chunks):
        if not old:
            ready.append(ref)
            copies.append([None] * count)
            continue
        n = ref.shape[1] // count
        parts = [(pl.ds(0, ref.shape[0]), pl.ds(n * c, n)) for c in range(count)]
        ready.append(buffers[at])
        copies.append([pltpu.make_async_copy(ref.at[p], buffers[at].at[p], sems.at[at, c]) for c, p in enumerate(parts)])
        at += 1
    for c in range(max(chunks)):
        for mine in copies:
            if c < len(mine) and mine[c] is not None:
                mine[c].start()
    return ready, copies


def arrive(copies):
    for copy in copies:
        if copy is not None:
            copy.wait()


def old_call(name, body, outs, out_specs, operands, olds, chunks, spot, scratch, mib):
    buffers = [pltpu.VMEM(a.shape, a.dtype) for a, old in zip(operands, olds) if old]
    n_in, n_old = len(operands), len(buffers)

    def inner(spot_ref, *refs):
        out_refs = refs[n_in : n_in + len(outs)]
        rest = refs[n_in + len(outs) :]
        ready, copies = fetched(refs[:n_in], olds, rest[:n_old], rest[n_old], chunks)
        body(spot_ref, ready, copies, out_refs, rest[n_old + 1 :])

    args = [pltpu.with_memory_space_constraint(a, pltpu.HBM) if old else a for a, old in zip(operands, olds)]
    return pl.pallas_call(
        inner,
        in_specs=[pl.BlockSpec(memory_space=pltpu.SMEM)]
        + [pl.BlockSpec(memory_space=pl.ANY if old else pltpu.VMEM) for old in olds],
        out_specs=out_specs,
        out_shape=outs,
        scratch_shapes=[*buffers, pltpu.SemaphoreType.DMA((max(n_old, 1), max(chunks))), *scratch],
        compiler_params=pltpu.CompilerParams(vmem_limit_bytes=mib * 2**20),
        cost_estimate=pl.CostEstimate(flops=2**32, bytes_accessed=2**23, transcendentals=0),
        name=name,
    )(spot, *args)


def term_body(spot, operands, copies, outs, scratch):
    turned, parts, sems = scratch
    for i in range(4):
        arrive(copies[i])
        turned[:, TOK * i : TOK * i + TOK] = operands[i][...].T
    sent = []
    for step in range(4):
        at = slice(512 * step, 512 * step + 512)
        arrive([copies[4 + i][step] for i in range(4)])
        total = None
        for i in range(4):
            part = dot_t(turned[:, TOK * i : TOK * i + TOK], operands[4 + i][:, at])
            total = part if total is None else total + part
        if step > 1:
            sent[step - 2].wait()
        parts[step & 1] = total.astype(LOW)
        sent.append(pltpu.make_async_copy(parts.at[step & 1], outs[0].at[:, pl.ds(512 * step, 512)], sems.at[step & 1]))
        sent[-1].start()
    arrive(sent[2:])


def weight_term(spot, lefts, rights, olds):
    return old_call(
        "weight_term",
        term_body,
        [pltpu.HBM((1024, 2048), LOW)],
        [pl.BlockSpec(memory_space=pl.ANY)],
        [*lefts, *rights],
        olds,
        [1] * 4 + [4] * 4,
        spot,
        [pltpu.VMEM((1024, 1024), LOW), pltpu.VMEM((2, 1024, 512), LOW), pltpu.SemaphoreType.DMA((2,))],
        16,
    )[0]


def head_terms_body(spot, operands, copies, outs, turned):
    rights = operands[4:8], operands[12:16]
    for g in range(2):
        for i in range(4):
            arrive(copies[8 * g + i])
            for x in range(4):
                for ylo in range(2):
                    at, to = 512 * ylo + 128 * x, 256 * x + 128 * ylo
                    turned[g][to : to + 128, TOK * i : TOK * i + TOK] = operands[8 * g + i][:, at : at + 128].T
    for i in (*range(4, 8), *range(12, 16)):
        arrive(copies[i])
    for slot in range(4):
        first = 1024 * (slot & 1)
        for g, width in enumerate((384, 128)):
            total = None
            for i in range(4):
                part = dot_t(turned[g][:, TOK * i : TOK * i + TOK], rights[g][i][:, width * slot : width * slot + width])
                total = part if total is None else total + part
            to = first + width * (slot >> 1)
            outs[0][:, to : to + width] = total.astype(LOW)
            first += 2 * width
    line = [jnp.sum(rights[0][i][...].astype(F32), axis=0, keepdims=True) for i in (0, 2)]
    outs[1][...] = line[0] + line[1]


def head_terms(spot, sides, olds):
    return old_call(
        "head_terms",
        head_terms_body,
        [shape((1024, 2048)), shape((1, 1536), F32)],
        [pl.BlockSpec(memory_space=pltpu.VMEM)] * 2,
        [part for side in sides for part in side],
        olds,
        [1] * 16,
        spot,
        [pltpu.VMEM((1024, 1024), LOW)] * 2,
        20,
    )


def cut_body(spot, total, *outs):
    for d in range(4):
        outs[d][...] = total[at_block((d & 1) ^ spot[2], 128), 1024 * (d >> 1) : 1024 * (d >> 1) + 1024]


def cut(spot, total):
    return call("cut", cut_body, [shape((128, 1024))] * 4, total, spot=spot)


def heads_result_body(p0, p1, p2, p3, q, k, v, o):
    total = four((p0, p1, p2, p3), slice(None))
    for j in range(2):
        to = slice(128 * j, 128 * j + 128)
        for t, ref in enumerate((q, k, v)):
            at = 384 * j + 128 * t
            ref[:, to] = total[:, at : at + 128]
        o[to] = total[:, 768 + 128 * j : 896 + 128 * j].T


def heads_result(parts):
    square = shape((128, 256), F32)
    return call("heads_result", heads_result_body, [square, square, square, shape((256, 128), F32)], *parts)


def hidden_result_body(up, up_far, down, down_far, up_out, down_out):
    up_out[...] = up[:, :1024].astype(F32) + up_far[...].astype(F32)
    down_out[...] = (down[:, :1024].astype(F32) + down_far[...].astype(F32)).T


def hidden_result(*parts):
    return call("hidden_result", hidden_result_body, [shape((128, 1024), F32), shape((1024, 128), F32)], *parts)


def norm_body(given, *refs):
    parts, (base, bias, gain, shift, normed, scale, result, low) = refs[:given], refs[given:]
    values = base[...] + bias[...] + ((parts[0][...] + parts[2][...].astype(F32)) + (parts[1][...].astype(F32) + parts[3][...].astype(F32)))
    center = jnp.mean(values, axis=-1, keepdims=True)
    centered = values - center
    spread = jnp.mean(centered * centered, axis=-1, keepdims=True)
    root = lax.rsqrt(spread + EPSILON)
    unit = centered * root
    normed[...] = unit
    scale[...] = root
    values = unit * gain[...] + shift[...]
    result[...] = values
    low[...] = values.astype(LOW)


def norm(parts, base, bias, gain, shift):
    rows = shape((OWN, D), F32)
    outs = [rows, shape((OWN, 1), F32), rows, shape((OWN, D))]
    return call("norm", functools.partial(norm_body, 4), outs, *parts, base, bias, gain, shift, flops=2**21)


def norm_back_body(given, under, *refs):
    parts, (base, normed, scale, gain, *refs) = refs[:given], refs[given:]
    if under:
        ffn_sums, sums_two, *refs = refs
    back, low, sums = refs
    grad = base[...]
    if given:
        grad = grad + ((parts[0][...] + parts[2][...].astype(F32)) + (parts[1][...].astype(F32) + parts[3][...].astype(F32)))
    unit = normed[...]
    tilted = grad * gain[...]
    values = tilted - jnp.mean(tilted, axis=-1, keepdims=True) - unit * jnp.mean(tilted * unit, axis=-1, keepdims=True)
    values = values * scale[...]
    back[...] = values
    cut = values.astype(LOW)
    low[:OWN] = cut
    lines = [jnp.sum(part, axis=0, keepdims=True) for part in (grad * unit, grad, cut.astype(F32))]
    for i, line in enumerate(lines):
        sums[i : i + 1] = line
    if under:
        lines = jnp.concatenate([*lines, ffn_sums[...], jnp.zeros((10, D), F32)], axis=0)
        both = jnp.concatenate([sums_two[...], jnp.zeros((10, D), F32)], axis=0)
        low[OWN:] = (lines + both).astype(LOW)


def norm_back(parts, base, normed, scale, gain, under=()):
    outs = [shape((OWN, D), F32), shape((OWN + 16 * bool(under), D)), shape((3, D), F32)]
    body = functools.partial(norm_back_body, len(parts), bool(under))
    return call("norm_back", body, outs, *parts, base, normed, scale, gain, *under, flops=2**21)


def marks_body(spot, seg, row, column, table):
    lane = lax.broadcasted_iota(jnp.int32, (1, 64), 1)
    for i in range(32):
        block = ((spot[1] ^ (i >> 4)) * 4 + (spot[0] ^ ((i >> 2) & 3))) * 4 + (spot[3] ^ (i & 3))
        line = seg[pl.ds(block, 1)] * 8192.0 + (block * 64 + lane).astype(F32)
        table[i : i + 1] = line
        if i < 16:
            row[:, 64 * i : 64 * i + 64] = line
    turned = table[...].T
    for i in range(32):
        column[64 * i : 64 * i + 64] = turned[:, i : i + 1]


def marks(spot, seg):
    outs = [shape((1, 1024), F32), shape((2048, 1), F32)]
    return call("marks", marks_body, outs, seg.reshape(32, 64), spot=spot, scratch=[pltpu.VMEM((32, 64), F32)])


def near(marks, keys, windowed):
    return jnp.abs(marks - keys) <= (REACH if windowed else 2047.0)


def load_heads(pieces, keys, values):
    for i, piece in enumerate(pieces):
        at = slice(TOK * i, TOK * i + TOK)
        keys[at] = piece[:, HD : 2 * HD]
        values[at] = piece[:, 2 * HD :]


def block_gap(spot, d, e):
    query, key = spot[0] ^ d, spot[0] ^ (e & 3)
    gap = jnp.abs(query - key)
    if e < 4:
        return gap
    return jnp.where(spot[1] == 0, 4 + key - query, 4 + query - key)


def attend_chunk(windowed, query, keys, at, qmark, kmark):
    s = dot_t(keys[at], query, 1, 1)
    return jnp.where(near(qmark, kmark[at], windowed), s, BLOCKED)


def fwd_body(windowed, spot, *refs):
    pieces, qmark, kmark = refs[:8], refs[8], refs[9]
    outs, lse, keys, values, best, total, mixed = refs[10:14], *refs[14:]
    load_heads(pieces, keys, values)
    own = slice(0, 4 * TOK if windowed else 8 * TOK)
    for d in range(4):
        at = slice(TOK * d, TOK * d + TOK)
        query, mark = pieces[d][:, :HD], qmark[:, at]
        s = attend_chunk(windowed, query, keys, own, mark, kmark)
        top = jnp.max(s, axis=0, keepdims=True)
        p = jnp.exp2((s - top) * (SCALE * LOG2E))
        count = jnp.sum(p, axis=0, keepdims=True)
        part = dot_t(values[own], p.astype(LOW), 0, 0)
        if windowed:
            best[...], total[...], mixed[...] = top, count, part
            for e in range(4, 8):

                @pl.when(block_gap(spot, d, e) < 3)
                def _():
                    far = slice(TOK * e, TOK * e + TOK)
                    s = attend_chunk(windowed, query, keys, far, mark, kmark)
                    top = jnp.maximum(best[...], jnp.max(s, axis=0, keepdims=True))
                    p = jnp.exp2((s - top) * (SCALE * LOG2E))
                    less = jnp.exp2((best[...] - top) * (SCALE * LOG2E))
                    total[...] = total[...] * less + jnp.sum(p, axis=0, keepdims=True)
                    mixed[...] = mixed[...] * less + dot_t(values[far], p.astype(LOW), 0, 0)
                    best[...] = top

            top, count, part = best[...], total[...], mixed[...]
        outs[d][...] = (part / count).T.astype(LOW)
        lse[:, at] = top * (SCALE * LOG2E) + jnp.log2(count)


def attend_fwd(spot, pieces, mark, windowed):
    n = 4 * TOK
    *mixed, lse = call(
        "attend_fwd",
        functools.partial(fwd_body, windowed),
        [shape((TOK, HD))] * 4 + [shape((1, n), F32)],
        *pieces,
        *mark,
        spot=spot,
        scratch=[pltpu.VMEM((2 * n, HD), LOW)] * 2
        + [pltpu.VMEM((1, TOK), F32)] * 2
        + [pltpu.VMEM((HD, TOK), F32)],
        mib=12,
        flops=8 * n * n * HD,
        size=2**22,
        exps=2 * n * n,
    )
    return mixed, lse


def bwd_body(windowed, spot, refs, copies, results, scratch):
    pieces, grads, outs, lse, qmark, kmark = refs[:8], refs[8:12], refs[12:16], *refs[16:]
    (*dq, own, far), (keys, values, acc, turned) = results, scratch
    n = 4 * TOK
    for copy in copies:
        arrive(copy)
    load_heads(pieces, keys, values)
    acc[...] = jnp.zeros_like(acc)
    for d in range(4):
        place = slice(TOK * d, TOK * d + TOK)
        query, grad, mark, norm_log = pieces[d][:, :HD], grads[d][...], qmark[:, place], lse[:, place]
        dots = jnp.sum((grad.astype(F32) * outs[d][...].astype(F32)).T, axis=0, keepdims=True)

        def chunk(at):
            s = attend_chunk(windowed, query, keys, at, mark, kmark)
            p = jnp.exp2(s * (SCALE * LOG2E) - norm_log)
            ds = (p * (dot_t(values[at], grad, 1, 1) - dots)).astype(LOW)
            acc[at, :HD] += dot_t(ds, query)
            acc[at, HD:] += dot_t(p.astype(LOW), grad)
            return dot_t(keys[at], ds, 0, 0)

        if not windowed:
            part = chunk(slice(0, 2 * n))
        else:
            turned[...] = chunk(slice(0, n))
            for e in range(4, 8):

                @pl.when(block_gap(spot, d, e) < 3)
                def _():
                    turned[...] += chunk(slice(TOK * e, TOK * e + TOK))

            part = turned[...]
        dq[d][...] = (part * SCALE).T.astype(LOW)
    for ref, start in ((own, 0), (far, n)):
        ref[:, :HD] = acc[start : start + n, :HD] * SCALE
        ref[:, HD:] = acc[start : start + n, HD:]


def attend_bwd(spot, pieces, grads, mixed, lse, mark, windowed):
    n = 4 * TOK
    old = [windowed] * 8
    outs = [shape((TOK, HD))] * 4 + [shape((n, 2 * HD), F32)] * 2
    *dq, own, far = old_call(
        "attend_bwd",
        functools.partial(bwd_body, windowed),
        outs,
        [pl.BlockSpec(memory_space=pltpu.VMEM)] * 6,
        [*pieces, *grads, *mixed, lse, *mark],
        old + [False] * 4 + old[:4] + [False] * 3,
        [1] * 19,
        spot,
        [pltpu.VMEM((2 * n, HD), LOW)] * 2 + [pltpu.VMEM((2 * n, 2 * HD), F32), pltpu.VMEM((HD, TOK), F32)],
        18,
    )
    return dq, own, far


def join_body(*refs):
    dq, own, far, outs = refs[:4], refs[4], refs[5], refs[6:]
    for d in range(4):
        at = slice(TOK * d, TOK * d + TOK)
        outs[d][:, :HD] = dq[d][...]
        outs[d][:, HD:] = (own[at] + far[at]).astype(LOW)


def join_heads(dq, own, far):
    return call("join_heads", join_body, [shape((TOK, 3 * HD))] * 4, *dq, own, far)


def swap(values, axis, bits, size=4):
    if axis == Y:
        bits = (bits & 1) * 2 + (bits >> 1)
    return lax.ppermute(values, axis, [(i, i ^ bits) for i in range(size)])


def sibling(values):
    return swap(values, "core", 1, 2)


def exchange(pieces, axis):
    got = {d: swap(pieces[d], axis, d) for d in (2, 1, 3)}
    return [pieces[0], got[1], got[2], got[3]]


def gather(piece, axis):
    return exchange([piece] * 4, axis)


def four_sum(parts):
    return (parts[0].astype(F32) + parts[2].astype(F32)) + (parts[1].astype(F32) + parts[3].astype(F32))


def line_sum(values, axis):
    return four_sum(gather(values, axis))


def tie(*values):
    return lax.optimization_barrier(values)


def pick(stacked, index):
    return lax.dynamic_index_in_dim(stacked, index, 0, keepdims=False)


def layer_forward(spot, stream, pieces, matrices, vectors, mark, windowed):
    heads_matrix, up_matrix, down_matrix = matrices
    qkv_bias, up_bias, out_bias, down_bias, attn_gain, attn_shift, ffn_gain, ffn_shift = vectors
    keep, send, *heads = rows_mm("qkv", spot, pieces, heads_matrix, qkv_bias)
    rows = (keep, send)
    heads = exchange(heads, "x")
    heads = heads + [sibling(h) for h in heads]
    mixed, lse = attend_fwd(spot, heads, mark, windowed)
    *branch, attended = scatter_mm(spot, exchange(mixed, "x"), heads_matrix, 512, 1536)
    normed, scale, first, low = norm(exchange(branch, "z"), stream, out_bias, attn_gain, attn_shift)
    loaded = load(up_matrix) if windowed else up_matrix
    keep, send, active, slope = rows_mm("up", spot, gather(low, "z"), loaded, up_bias)
    if windowed:
        down_matrix = load(up_matrix, 2048)
    second = scatter_mm(spot, [active], down_matrix, 2048, 0)
    normed_two, scale_two, result, low = norm(exchange(second, "z"), first, down_bias, ffn_gain, ffn_shift)
    saved = (heads, mixed, lse, normed, scale, slope, normed_two, scale_two)
    far = [sibling(part) for part in (rows[1], attended, send, active)]
    low, *far = tie(low, *far)
    sides = (rows[0], far[0]), (attended, far[1]), (keep, far[2]), (active, far[3])
    return result, low, saved, sides, (heads_matrix, loaded, down_matrix)


FRESH_LEFTS = [False] * 2 + [True] * 6
FRESH_RIGHTS = [True] * 4 + [False] * 2 + [True] * 2


def layer_backward(spot, parts, base, saved, sides, matrices, vectors, mark, windowed, earlier=None, before=(), sums_two=None, turn=None):
    heads_matrix, up_matrix, down_matrix = matrices
    attn_gain, ffn_gain = vectors[4], vectors[6]
    heads, mixed, lse, normed, scale, slope, normed_two, scale_two = saved
    rows, attended, first_rows, active = sides
    last = earlier is not None
    grad_summed, low, ffn_sums = norm_back(parts, base, normed_two, scale_two, ffn_gain)
    keep, send, grad_up, up_sums = rows_mm("slope", spot, gather(low, "z"), down_matrix, slope)
    down_pair = (keep, sibling(send)), active
    up_pair = first_rows, (grad_up, sibling(grad_up))
    if last:
        down_term = weight_term(spot, *two_layers(down_pair, earlier[3]), FRESH_LEFTS)
        grad_up, down_term = tie(grad_up, down_term)
    parts = exchange(scatter_mm(spot, [grad_up], up_matrix, 2048, 0), "z")
    if last:
        down_sum = lax.psum_scatter(down_term, ("ylo", "x"), scatter_dimension=0, tiled=True)
        up_term = weight_term(spot, *two_layers(up_pair, earlier[2]), FRESH_RIGHTS)
    under = (ffn_sums, sums_two[0]) if last else ()
    grad_residual, low, attn_sums = norm_back(parts, grad_summed, normed, scale, attn_gain, under)
    if last:
        low, up_term = tie(low, up_term)
        up_sum = lax.psum_scatter(up_term, ("ylo", "x"), scatter_dimension=0, tiled=True)
    sums = (jnp.concatenate([attn_sums, ffn_sums]), up_sums)
    keep, send, *grad_heads = rows_mm("heads", spot, gather(low, "z"), heads_matrix)
    if last:
        *grad_heads, own_sums = grad_heads
        hidden_sums = by_yhi((up_sums + sums_two[1]).reshape(2, 1024), spot[4])
        sums = jnp.concatenate([own_sums[:6].reshape(24, 512), hidden_sums.reshape(4, 512)])
    out_pair = (keep, sibling(send)), attended
    grad_heads = exchange(grad_heads, "x")
    grad_heads[3], *before = tie(grad_heads[3], *before)
    grad_queries, own_terms, far_terms = attend_bwd(spot, heads, grad_heads, mixed, lse, mark, windowed)
    grad_parts = exchange(join_heads(grad_queries, own_terms, sibling(far_terms)), "x")
    *partial, grad_packed = scatter_mm(spot, grad_parts, heads_matrix, 1536, 0)
    qkv_pair = rows, (grad_packed, sibling(grad_packed))
    if not last:
        return exchange(partial, "z"), grad_residual, (qkv_pair, out_pair, up_pair, down_pair), sums, before
    sides = [*two_layers(qkv_pair, earlier[0]), *two_layers(out_pair, earlier[1])]
    rest, line = head_terms(spot, sides, FRESH_RIGHTS + FRESH_LEFTS)
    rest, line, *partial = tie(rest, line, *partial)
    rest = lax.psum_scatter(rest, "x", scatter_dimension=0, tiled=True)
    low = (four_sum(exchange(partial, "z")) + grad_residual).astype(LOW)
    same, other = turn(low)
    heads = line.reshape(2, 2, 3, 128)
    heads = jnp.stack([by_yhi(heads[j], spot[4]) for j in range(2)]).reshape(3, 512)
    sums = jnp.concatenate([sums, heads, jnp.zeros((1, 512), F32)])
    sums = line_sum(line_sum(sums + sibling(sums), "x"), Y).reshape(-1)
    result = gather(by_micro(spot[4], same, other), "z")
    far = [swap(total[:, 1024:], "yhi", 1, 2) for total in (up_sum, down_sum)]
    rest, *far = tie(rest, *far)
    rest = heads_result(exchange(cut(spot, rest), Y))
    return settle(spot, result), (*rest, *hidden_result(up_sum, far[0], down_sum, far[1])), sums


def two_layers(one, two):
    return list(one[0]) + list(two[0]), list(one[1]) + list(two[1])


def turn_same(core, ylo, values):
    got = lax.ppermute(values, ("core", "ylo"), [(1, 2), (2, 1)])
    return jnp.where(core == ylo, values, got)


def turn_other(values):
    perm = [(c * 4 + l * 2 + h, l * 4 + c * 2 + 1 - h) for c in range(2) for l in range(2) for h in range(2)]
    return lax.ppermute(values, ("core", "ylo", "yhi"), perm)


def by_micro(yhi, same, other):
    return jnp.stack([jnp.where(yhi == 0, same, other), jnp.where(yhi == 0, other, same)])


def by_yhi(values, yhi):
    return jnp.where(yhi == 0, values, values[::-1])


def shards(
    inputs,
    cotangent,
    segments,
    query_weight,
    key_weight,
    value_weight,
    out_weight,
    up_weight,
    down_weight,
    query_bias,
    value_bias,
    out_bias,
    up_bias,
    down_bias,
    attn_gain,
    attn_shift,
    ffn_gain,
    ffn_shift,
):
    core, ylo, x, yhi, z = (lax.axis_index(name) for name in AXES)
    spot = jnp.stack([x, core, ylo, z, yhi]).astype(jnp.int32)
    local = pack(pack_heads_body, 1024, query_weight, key_weight, value_weight, out_weight)
    parts = gather(local, Y)
    *parts, inputs, down_weight = tie(*parts, inputs, down_weight)

    def gathered(heads, parts):
        return lax.all_gather(pair(heads, spot, parts), ("core", "x"), axis=0, tiled=True)

    heads_matrix = gathered(True, parts)
    own_rows = turn_same(core, ylo, pick(pick(inputs, yhi)[0].reshape(4, OWN, D), z))
    pieces = gather(own_rows, "z")
    *pieces, up_weight = tie(*pieces, up_weight)
    hidden_matrix = gathered(False, gather(up_weight, Y) + gather(pack(turn_body, 1024, down_weight), Y))
    matrices = (load(heads_matrix), hidden_matrix, None)
    bias_own = jnp.concatenate([query_bias, value_bias, up_bias])
    bias = (bias_own, swap(bias_own, "yhi", 1, 2))
    none = jnp.zeros((128,), F32)
    qkv_bias = jnp.concatenate(
        [
            part
            for j in range(2)
            for h in range(2)
            for part in (bias[h][128 * j : 128 * j + 128], none, bias[h][256 + 128 * j : 384 + 128 * j])
        ]
    )
    up_all = jnp.concatenate([bias[h][512:] for h in range(2)])
    vectors = (qkv_bias, up_all, out_bias, down_bias, attn_gain, attn_shift, ffn_gain, ffn_shift)
    vectors = tuple(v[None] for v in vectors)
    top_grad = turn_same(core, ylo, pick(pick(cotangent, yhi)[0].reshape(4, OWN, D), z)).astype(F32)
    seg_here = pick(segments, yhi)[0].astype(F32)
    mark = marks(spot, jnp.where(core == ylo, seg_here, sibling(seg_here)))
    middle, low, saved_one, sides_one, matrices = layer_forward(
        spot, own_rows.astype(F32), pieces, matrices, vectors, mark, True
    )
    _, low, saved_two, sides_two, _ = layer_forward(spot, middle, gather(low, "z"), matrices, vectors, mark, False)
    parts, base, pairs, sums_two, result = layer_backward(
        spot, [], top_grad, saved_two, sides_two, matrices, vectors, mark, False, None, gather(low, "z")
    )
    result = settle(spot, result)
    same, other = turn_same(core, ylo, result), turn_other(result)
    parts[0], same, other = tie(parts[0], same, other)

    def turn(low):
        return turn_same(core, ylo, low), turn_other(low)

    input_grad, matrix_grads, sums = layer_backward(
        spot, parts, base, saved_one, sides_one, matrices, vectors, mark, True, pairs, (), sums_two, turn
    )
    own = sums[: 6 * D].reshape(6, D)
    heads = sums[7 * D : 7 * D + 1536].reshape(2, 2, 3, 128)
    heads = lax.dynamic_index_in_dim(heads, yhi, 1, keepdims=False)
    return (
        by_micro(yhi, same, other)[:, None],
        input_grad[:, None],
        *matrix_grads,
        heads[:, 0].reshape(-1),
        heads[:, 2].reshape(-1),
        own[2],
        pick(sums[6 * D : 7 * D].reshape(2, 1024), yhi),
        own[5],
        own[0],
        own[1],
        own[3],
        own[4],
    )


def solution(mesh):
    split = Mesh(mesh.devices.reshape(2, 2, 4, 2, 4), AXES)
    token = P(None, "core", ("ylo", "x"), None)
    inner = P(("core", "ylo", "x"), ("yhi", "z"))
    outer = P(("yhi", "z"), ("core", "ylo", "x"))
    unit = P(("yhi", "z"))
    matrix = (inner, inner, inner, outer, inner, outer)
    vector = (unit, unit, P(), unit, P(), P(), P(), P(), P())
    in_specs = (token, token, P(None, "core", None)) + matrix + vector
    out_specs = (token, token) + matrix + vector
    return jax.shard_map(shards, mesh=split, in_specs=in_specs, out_specs=out_specs, check_vma=False)
```

```python
import functools

import jax
import jax.numpy as jnp
from jax import lax
from jax.experimental import pallas as pl
from jax.experimental.pallas import tpu as pltpu
from jax.sharding import Mesh, PartitionSpec as P

AXES = ("core", "ylo", "x", "yhi", "z")
Y = ("ylo", "yhi")
ROWS = ("core", "ylo", "x")
D = 2048
HD = 128
TOK = 256
OWN = 64
REACH = 512
LOW = jnp.bfloat16
F32 = jnp.float32
BLOCKED = -1e30
SCALE = HD ** (-0.5)
LOG2E = 1.4426950408889634
EPSILON = 1e-05
CURVE = 0.7978845608028654
CUBIC = 0.044715


def shape(dims, dtype=LOW):
    return jax.ShapeDtypeStruct(dims, dtype)


def dot_t(a, b, ca=1, cb=0):
    return lax.dot_general(a, b, (((ca,), (cb,)), ((), ())), preferred_element_type=F32)


def call(name, body, outs, *args, spot=None, scratch=(), mib=12, flops=0, size=2**21, exps=0):
    specs = [pl.BlockSpec(memory_space=pltpu.VMEM)] * len(args)
    if spot is not None:
        args = (spot,) + args
        specs = [pl.BlockSpec(memory_space=pltpu.SMEM)] + specs
    return pl.pallas_call(
        body,
        in_specs=specs,
        out_specs=[pl.BlockSpec(memory_space=pltpu.VMEM)] * len(outs),
        out_shape=outs,
        scratch_shapes=scratch,
        compiler_params=pltpu.CompilerParams(vmem_limit_bytes=mib * 2**20),
        cost_estimate=pl.CostEstimate(flops=flops, bytes_accessed=size, transcendentals=exps),
        name=name,
    )(*args)


def at_block(index, size):
    return pl.ds(pl.multiple_of(index * size, size), size)


def pack_heads_body(q_far, k_far, v_far, o_far, out, q, k, v, o, sems):
    copies = [
        pltpu.make_async_copy(far, part, sems.at[i])
        for i, (far, part) in enumerate(((q_far, q), (k_far, k), (v_far, v), (o_far, o)))
    ]
    for copy in copies:
        copy.start()
    for copy in copies:
        copy.wait()
    for j in range(2):
        at = slice(128 * j, 128 * j + 128)
        for t, part in enumerate((q, k, v)):
            out[:, 384 * j + 128 * t : 384 * j + 128 * t + 128] = part[:, at]
    out[:, 768:] = o[...].T


def pack_heads(*parts):
    return pl.pallas_call(
        pack_heads_body,
        in_specs=[pl.BlockSpec(memory_space=pl.ANY)] * 4,
        out_specs=pl.BlockSpec(memory_space=pltpu.VMEM),
        out_shape=shape((128, 1024)),
        scratch_shapes=[pltpu.VMEM(part.shape, part.dtype) for part in parts] + [pltpu.SemaphoreType.DMA((4,))],
        compiler_params=pltpu.CompilerParams(vmem_limit_bytes=2**22),
        cost_estimate=pl.CostEstimate(flops=0, bytes_accessed=2**19, transcendentals=0),
        name="pack_heads",
    )(*[pltpu.with_memory_space_constraint(part, pltpu.HBM) for part in parts])


def turn_body(down, out):
    out[...] = down[...].T


def join_heads_columns(own, far, out, rows):
    for j in range(2):
        for h, part in enumerate((own, far)):
            slot = 2 * j + h
            out[rows, 384 * slot : 384 * slot + 384] = part[:, 384 * j : 384 * j + 384]
            out[rows, 1536 + 128 * slot : 1664 + 128 * slot] = part[:, 768 + 128 * j : 896 + 128 * j]


def pair_body(heads, spot, *refs):
    parts, out = refs[:-1], refs[-1]
    for ylo in range(2):
        rows = at_block(ylo ^ spot[2], 128)
        if heads:
            join_heads_columns(parts[ylo], parts[ylo + 2], out, rows)
            continue
        for i, d in enumerate((ylo, ylo + 2, ylo + 4, ylo + 6)):
            out[rows, 1024 * i : 1024 * i + 1024] = parts[d][...]


def pair(heads, spot, parts):
    outs = [shape((256, 2048 if heads else 4096))]
    return call("pair", functools.partial(pair_body, heads), outs, *parts, spot=spot)[0]


def pack(body, width, *parts):
    return call("pack", body, [shape((128, width))], *parts)[0]


def turned_rows(source, kept, columns, to, sems):
    copies = []
    for core in range(2):
        for ylo in range(2):
            for x in range(4):
                at, row = 256 * (4 * core + x) + 128 * ylo, 1024 * core + 512 * ylo + 128 * x
                part = source.at[pl.ds(at, 128), pl.ds(columns[0], columns[1])]
                place = kept.at[pl.ds(row, 128), pl.ds(to, columns[1])]
                copies.append(pltpu.make_async_copy(part, place, sems.at[len(copies)]))
    return copies


def held(matrix):
    return pltpu.with_memory_space_constraint(matrix, pltpu.VMEM)


def settle_body(spot, p0, p1, p2, p3, out):
    for d, part in enumerate((p0, p1, p2, p3)):
        at = at_block(d ^ spot[3], OWN)
        if len(out.shape) == 2:
            out[at] = part[...]
        else:
            out[:, at] = part[...]


def settle(spot, parts):
    return call("settle", settle_body, [shape(parts[0].shape[:-2] + (TOK, D))], *parts, spot=spot)[0]


def four(refs, at):
    p = [ref[at].astype(F32) for ref in refs]
    return (p[0] + p[2]) + (p[1] + p[3])


def rows_body(kind, first, loads, spot, p0, p1, p2, p3, w, *refs):
    extra = refs[0] if kind != "heads" else None
    keep, send, *outs = refs[1:] if kind != "heads" else refs
    chunks, later = [], []
    if loads:
        source = w
        *outs, sems = outs
        w, *more = outs[-loads:]
        outs = outs[:-loads]
        chunks = [turned_rows(source, w, (512 * c, 512), 512 * c, sems.at[c]) for c in range(4)]
        later = [turned_rows(source, ref, (2048, 2048), 0, sems.at[4]) for ref in more]
        for chunk in chunks + later:
            for copy in chunk:
                copy.start()

    def loaded(count):
        while chunks and 4 - len(chunks) < count:
            for copy in chunks.pop(0):
                copy.wait()

    kept, sent = at_block(spot[1], D // 2), at_block(1 - spot[1], D // 2)
    for i, p in enumerate((p0, p1, p2, p3)):
        keep[OWN * i : OWN * i + OWN] = p[:OWN, kept]
        send[OWN * i : OWN * i + OWN] = p[:OWN, sent]
    if p0.shape[0] > OWN:
        *outs, sums = outs
        sums[...] = four((p0, p1, p2, p3), slice(OWN, OWN + 16))

    def product(at):
        return dot_t(keep[...], w[kept, at]) + dot_t(send[...], w[sent, at])

    if kind == "qkv" and loads:
        for slot in range(4):
            loaded(slot if slot else 1)
            low = (product(slice(384 * slot, 384 * slot + 384)) + extra[:, 384 * slot : 384 * slot + 384]).astype(LOW)
            for d in range(4):

                @pl.when((slot ^ spot[0]) == d)
                def _():
                    outs[d][...] = low

        loaded(4)
        return
    if kind in ("qkv", "heads"):
        width = outs[0].shape[1]
        for d in range(4):
            slot = d ^ spot[0]
            values = product(pl.ds(pl.multiple_of(first + slot * width, 128), width))
            if kind == "qkv":
                values = values + extra[:, at_block(slot, width)]
            outs[d][...] = values.astype(LOW)
        return
    tile = 512
    for i in range(4):
        at = slice(tile * i, tile * i + tile)
        loaded(i + 1)
        values = product(at)
        if kind == "up":
            values = values + extra[:, at]
            square = values * values
            bend = jnp.tanh(CURVE * (values + CUBIC * (square * values)))
            outs[0][:, at] = (0.5 * values * (1.0 + bend)).astype(LOW)
            slope = 0.5 * (1.0 + bend) + 0.5 * values * (1.0 - bend * bend) * (CURVE * (1.0 + 3.0 * CUBIC * square))
            outs[1][:, at] = slope.astype(LOW)
        else:
            low = (values * extra[:, at].astype(F32)).astype(LOW)
            outs[0][:, at] = low
            outs[1][:, at] = jnp.sum(low.astype(F32), axis=0, keepdims=True)
    for chunk in later:
        for copy in chunk:
            copy.wait()


def rows_mm(kind, spot, pieces, weight, extra=None, loads=0):
    half = shape((TOK, D // 2))
    n, first, outs = {
        "qkv": (1536, 0, [shape((TOK, 384))] * 4),
        "heads": (512, 1536, [shape((TOK, HD))] * 4),
        "up": (2048, 0, [shape((TOK, 2048))] * 2),
        "slope": (2048, 0, [shape((TOK, 2048)), shape((1, 2048), F32)]),
    }[kind]
    args = [weight if loads else held(weight)] + ([] if extra is None else [extra])
    if pieces[0].shape[0] > OWN:
        outs = [*outs, shape((16, D), F32)]
    body = functools.partial(rows_body, kind, first, loads)
    cost = pl.CostEstimate(flops=2 * TOK * D * n, bytes_accessed=2 * D * n, transcendentals=TOK * n if kind == "up" else 0)
    vmem = pl.BlockSpec(memory_space=pltpu.VMEM)
    if loads:
        args[0] = pltpu.with_memory_space_constraint(weight, pltpu.HBM)
    return pl.pallas_call(
        body,
        in_specs=[pl.BlockSpec(memory_space=pltpu.SMEM)]
        + [vmem] * 4
        + [pl.BlockSpec(memory_space=pl.ANY) if loads else vmem]
        + [vmem] * (len(args) - 1),
        out_specs=[vmem] * (2 + len(outs) + loads),
        out_shape=[half, half, *outs] + [pltpu.VMEM((D, 2048), LOW)] * loads,
        scratch_shapes=[pltpu.SemaphoreType.DMA((5, 16))] if loads else [],
        compiler_params=pltpu.CompilerParams(vmem_limit_bytes=12 * 2**20),
        cost_estimate=cost,
        name="rows_" + kind,
    )(spot, *pieces, *args)


def scatter_body(n_parts, first, k, spot, *refs):
    parts, w, outs = refs[:n_parts], refs[n_parts], refs[n_parts + 1 : n_parts + 5]
    if n_parts == 1:
        rows = parts[0]
    else:
        rows = refs[n_parts + 5]
        for d, part in enumerate(parts):
            rows[:, at_block(d ^ spot[0], k // 4)] = part[...]
    tile = 512
    for i in range(D // tile):
        to = slice(tile * i, tile * i + tile)
        values = dot_t(rows[...], w[to, first : first + k], 1, 1)
        outs[0][:, to] = values[:OWN]
        for d in range(1, 4):
            outs[d][:, to] = values[OWN * d : OWN * d + OWN].astype(LOW)


def scatter_mm(spot, parts, weight, k, first):
    outs = [shape((OWN, D), F32)] + [shape((OWN, D))] * 3
    if len(parts) > 1:
        outs.append(shape((TOK, k)))
    return call(
        "scatter_mm",
        functools.partial(scatter_body, len(parts), first, k),
        outs,
        *parts,
        held(weight),
        spot=spot,
        flops=2 * TOK * D * k,
        size=2 * D * k,
    )


def fetched(refs, olds, buffers, sems, chunks):
    ready, copies, at = [], [], 0
    for ref, old, count in zip(refs, olds, chunks):
        if not old:
            ready.append(ref)
            copies.append([None] * count)
            continue
        n = ref.shape[1] // count
        parts = [(pl.ds(0, ref.shape[0]), pl.ds(n * c, n)) for c in range(count)]
        ready.append(buffers[at])
        copies.append([pltpu.make_async_copy(ref.at[p], buffers[at].at[p], sems.at[at, c]) for c, p in enumerate(parts)])
        at += 1
    for c in range(max(chunks)):
        for mine in copies:
            if c < len(mine) and mine[c] is not None:
                mine[c].start()
    return ready, copies


def arrive(copies):
    for copy in copies:
        if copy is not None:
            copy.wait()


def old_call(name, body, outs, out_specs, operands, olds, chunks, spot, scratch, mib):
    buffers = [pltpu.VMEM(a.shape, a.dtype) for a, old in zip(operands, olds) if old]
    n_in, n_old = len(operands), len(buffers)

    def inner(spot_ref, *refs):
        out_refs = refs[n_in : n_in + len(outs)]
        rest = refs[n_in + len(outs) :]
        ready, copies = fetched(refs[:n_in], olds, rest[:n_old], rest[n_old], chunks)
        body(spot_ref, ready, copies, out_refs, rest[n_old + 1 :])

    args = [pltpu.with_memory_space_constraint(a, pltpu.HBM) if old else a for a, old in zip(operands, olds)]
    return pl.pallas_call(
        inner,
        in_specs=[pl.BlockSpec(memory_space=pltpu.SMEM)]
        + [pl.BlockSpec(memory_space=pl.ANY if old else pltpu.VMEM) for old in olds],
        out_specs=out_specs,
        out_shape=outs,
        scratch_shapes=[*buffers, pltpu.SemaphoreType.DMA((max(n_old, 1), max(chunks))), *scratch],
        compiler_params=pltpu.CompilerParams(vmem_limit_bytes=mib * 2**20),
        cost_estimate=pl.CostEstimate(flops=2**32, bytes_accessed=2**23, transcendentals=0),
        name=name,
    )(spot, *args)


def term_body(spot, operands, copies, outs, scratch):
    turned, parts, sems = scratch
    for i in range(4):
        arrive(copies[i])
        turned[:, TOK * i : TOK * i + TOK] = operands[i][...].T
    sent = []
    for step in range(4):
        at = slice(512 * step, 512 * step + 512)
        arrive([copies[4 + i][step] for i in range(4)])
        total = None
        for i in range(4):
            part = dot_t(turned[:, TOK * i : TOK * i + TOK], operands[4 + i][:, at])
            total = part if total is None else total + part
        if step > 1:
            sent[step - 2].wait()
        parts[step & 1] = total.astype(LOW)
        sent.append(pltpu.make_async_copy(parts.at[step & 1], outs[0].at[:, pl.ds(512 * step, 512)], sems.at[step & 1]))
        sent[-1].start()
    arrive(sent[2:])


def weight_term(spot, lefts, rights, olds):
    return old_call(
        "weight_term",
        term_body,
        [pltpu.HBM((1024, 2048), LOW)],
        [pl.BlockSpec(memory_space=pl.ANY)],
        [*lefts, *rights],
        olds,
        [1] * 4 + [4] * 4,
        spot,
        [pltpu.VMEM((1024, 1024), LOW), pltpu.VMEM((2, 1024, 512), LOW), pltpu.SemaphoreType.DMA((2,))],
        16,
    )[0]


def head_terms_body(spot, operands, copies, outs, scratch):
    *turned, parts, sems = scratch
    rights = operands[4:8], operands[12:16]
    for g in range(2):
        for i in range(4):
            arrive(copies[8 * g + i])
            for x in range(4):
                for ylo in range(2):
                    at, to = 512 * ylo + 128 * x, 256 * x + 128 * ylo
                    turned[g][to : to + 128, TOK * i : TOK * i + TOK] = operands[8 * g + i][:, at : at + 128].T
    for i in (*range(4, 8), *range(12, 16)):
        arrive(copies[i])
    sent = []
    for slot in range(4):
        if slot > 1:
            arrive(sent[2 * slot - 4 : 2 * slot - 2])
        first = 1024 * (slot & 1)
        at = 0
        for g, width in enumerate((384, 128)):
            total = None
            for i in range(4):
                part = dot_t(turned[g][:, TOK * i : TOK * i + TOK], rights[g][i][:, width * slot : width * slot + width])
                total = part if total is None else total + part
            held_part = parts.at[slot & 1, :, pl.ds(at, width)]
            held_part[...] = total.astype(LOW)
            to = first + width * (slot >> 1)
            sent.append(pltpu.make_async_copy(held_part, outs[0].at[:, pl.ds(to, width)], sems.at[slot & 1, g]))
            sent[-1].start()
            first += 2 * width
            at += width
    line = [jnp.sum(rights[0][i][...].astype(F32), axis=0, keepdims=True) for i in (0, 2)]
    outs[1][...] = line[0] + line[1]
    arrive(sent[4:])


def head_terms(spot, sides, olds):
    return old_call(
        "head_terms",
        head_terms_body,
        [pltpu.HBM((1024, 2048), LOW), shape((1, 1536), F32)],
        [pl.BlockSpec(memory_space=pl.ANY), pl.BlockSpec(memory_space=pltpu.VMEM)],
        [part for side in sides for part in side],
        olds,
        [1] * 16,
        spot,
        [pltpu.VMEM((1024, 1024), LOW)] * 2 + [pltpu.VMEM((2, 1024, 512), LOW), pltpu.SemaphoreType.DMA((2, 2))],
        20,
    )


def cut_body(spot, total, *outs):
    for d in range(4):
        outs[d][...] = total[at_block((d & 1) ^ spot[2], 128), 1024 * (d >> 1) : 1024 * (d >> 1) + 1024]


def cut(spot, total):
    return call("cut", cut_body, [shape((128, 1024))] * 4, total, spot=spot)


def heads_result_body(p0, p1, p2, p3, q, k, v, o):
    total = four((p0, p1, p2, p3), slice(None))
    for j in range(2):
        to = slice(128 * j, 128 * j + 128)
        for t, ref in enumerate((q, k, v)):
            at = 384 * j + 128 * t
            ref[:, to] = total[:, at : at + 128]
        o[to] = total[:, 768 + 128 * j : 896 + 128 * j].T


def heads_result(parts):
    square = shape((128, 256), F32)
    return call("heads_result", heads_result_body, [square, square, square, shape((256, 128), F32)], *parts)


def hidden_result_body(up, up_far, down, down_far, up_out, down_out):
    up_out[...] = up[:, :1024].astype(F32) + up_far[...].astype(F32)
    down_out[...] = (down[:, :1024].astype(F32) + down_far[...].astype(F32)).T


def hidden_result(*parts):
    return call("hidden_result", hidden_result_body, [shape((128, 1024), F32), shape((1024, 128), F32)], *parts)


def norm_body(given, *refs):
    parts, (base, bias, gain, shift, normed, scale, result, low) = refs[:given], refs[given:]
    values = base[...] + bias[...] + ((parts[0][...] + parts[2][...].astype(F32)) + (parts[1][...].astype(F32) + parts[3][...].astype(F32)))
    center = jnp.mean(values, axis=-1, keepdims=True)
    centered = values - center
    spread = jnp.mean(centered * centered, axis=-1, keepdims=True)
    root = lax.rsqrt(spread + EPSILON)
    unit = centered * root
    normed[...] = unit
    scale[...] = root
    values = unit * gain[...] + shift[...]
    result[...] = values
    low[...] = values.astype(LOW)


def norm(parts, base, bias, gain, shift):
    rows = shape((OWN, D), F32)
    outs = [rows, shape((OWN, 1), F32), rows, shape((OWN, D))]
    return call("norm", functools.partial(norm_body, 4), outs, *parts, base, bias, gain, shift, flops=2**21)


def norm_back_body(given, under, *refs):
    parts, (base, normed, scale, gain, *refs) = refs[:given], refs[given:]
    if under:
        ffn_sums, sums_two, *refs = refs
    back, low, sums = refs
    grad = base[...]
    if given:
        grad = grad + ((parts[0][...] + parts[2][...].astype(F32)) + (parts[1][...].astype(F32) + parts[3][...].astype(F32)))
    unit = normed[...]
    tilted = grad * gain[...]
    values = tilted - jnp.mean(tilted, axis=-1, keepdims=True) - unit * jnp.mean(tilted * unit, axis=-1, keepdims=True)
    values = values * scale[...]
    back[...] = values
    cut = values.astype(LOW)
    low[:OWN] = cut
    lines = [jnp.sum(part, axis=0, keepdims=True) for part in (grad * unit, grad, cut.astype(F32))]
    for i, line in enumerate(lines):
        sums[i : i + 1] = line
    if under:
        lines = jnp.concatenate([*lines, ffn_sums[...], jnp.zeros((10, D), F32)], axis=0)
        both = jnp.concatenate([sums_two[...], jnp.zeros((10, D), F32)], axis=0)
        low[OWN:] = (lines + both).astype(LOW)


def norm_back(parts, base, normed, scale, gain, under=()):
    outs = [shape((OWN, D), F32), shape((OWN + 16 * bool(under), D)), shape((3, D), F32)]
    body = functools.partial(norm_back_body, len(parts), bool(under))
    return call("norm_back", body, outs, *parts, base, normed, scale, gain, *under, flops=2**21)


def marks_body(spot, seg, row, column, table):
    lane = lax.broadcasted_iota(jnp.int32, (1, 64), 1)
    for i in range(32):
        block = ((spot[1] ^ (i >> 4)) * 4 + (spot[0] ^ ((i >> 2) & 3))) * 4 + (spot[3] ^ (i & 3))
        line = seg[pl.ds(block, 1)] * 8192.0 + (block * 64 + lane).astype(F32)
        table[i : i + 1] = line
        if i < 16:
            row[:, 64 * i : 64 * i + 64] = line
    turned = table[...].T
    for i in range(32):
        column[64 * i : 64 * i + 64] = turned[:, i : i + 1]


def marks(spot, seg):
    outs = [shape((1, 1024), F32), shape((2048, 1), F32)]
    return call("marks", marks_body, outs, seg.reshape(32, 64), spot=spot, scratch=[pltpu.VMEM((32, 64), F32)])


def near(marks, keys, windowed):
    return jnp.abs(marks - keys) <= (REACH if windowed else 2047.0)


def load_heads(pieces, keys, values):
    for i, piece in enumerate(pieces):
        at = slice(TOK * i, TOK * i + TOK)
        keys[at] = piece[:, HD : 2 * HD]
        values[at] = piece[:, 2 * HD :]


def block_gap(spot, d, e):
    query, key = spot[0] ^ d, spot[0] ^ (e & 3)
    gap = jnp.abs(query - key)
    if e < 4:
        return gap
    return jnp.where(spot[1] == 0, 4 + key - query, 4 + query - key)


def attend_chunk(windowed, query, keys, at, qmark, kmark):
    s = dot_t(keys[at], query, 1, 1)
    return jnp.where(near(qmark, kmark[at], windowed), s, BLOCKED)


def fwd_body(windowed, spot, *refs):
    pieces, qmark, kmark = refs[:8], refs[8], refs[9]
    outs, lse, keys, values, best, total, mixed = refs[10:14], *refs[14:]
    load_heads(pieces, keys, values)
    own = slice(0, 4 * TOK if windowed else 8 * TOK)
    for d in range(4):
        at = slice(TOK * d, TOK * d + TOK)
        query, mark = pieces[d][:, :HD], qmark[:, at]
        s = attend_chunk(windowed, query, keys, own, mark, kmark)
        top = jnp.max(s, axis=0, keepdims=True)
        p = jnp.exp2((s - top) * (SCALE * LOG2E))
        count = jnp.sum(p, axis=0, keepdims=True)
        part = dot_t(values[own], p.astype(LOW), 0, 0)
        if windowed:
            best[...], total[...], mixed[...] = top, count, part
            for e in range(4, 8):

                @pl.when(block_gap(spot, d, e) < 3)
                def _():
                    far = slice(TOK * e, TOK * e + TOK)
                    s = attend_chunk(windowed, query, keys, far, mark, kmark)
                    top = jnp.maximum(best[...], jnp.max(s, axis=0, keepdims=True))
                    p = jnp.exp2((s - top) * (SCALE * LOG2E))
                    less = jnp.exp2((best[...] - top) * (SCALE * LOG2E))
                    total[...] = total[...] * less + jnp.sum(p, axis=0, keepdims=True)
                    mixed[...] = mixed[...] * less + dot_t(values[far], p.astype(LOW), 0, 0)
                    best[...] = top

            top, count, part = best[...], total[...], mixed[...]
        outs[d][...] = (part / count).T.astype(LOW)
        lse[:, at] = top * (SCALE * LOG2E) + jnp.log2(count)


def attend_fwd(spot, pieces, mark, windowed):
    n = 4 * TOK
    *mixed, lse = call(
        "attend_fwd",
        functools.partial(fwd_body, windowed),
        [shape((TOK, HD))] * 4 + [shape((1, n), F32)],
        *pieces,
        *mark,
        spot=spot,
        scratch=[pltpu.VMEM((2 * n, HD), LOW)] * 2
        + [pltpu.VMEM((1, TOK), F32)] * 2
        + [pltpu.VMEM((HD, TOK), F32)],
        mib=12,
        flops=8 * n * n * HD,
        size=2**22,
        exps=2 * n * n,
    )
    return mixed, lse


def bwd_body(windowed, spot, refs, copies, results, scratch):
    pieces, grads, outs, lse, qmark, kmark = refs[:8], refs[8:12], refs[12:16], *refs[16:]
    (*dq, own, far), (keys, values, acc, turned) = results, scratch
    n = 4 * TOK
    for copy in copies:
        arrive(copy)
    load_heads(pieces, keys, values)
    acc[...] = jnp.zeros_like(acc)
    for d in range(4):
        place = slice(TOK * d, TOK * d + TOK)
        query, grad, mark, norm_log = pieces[d][:, :HD], grads[d][...], qmark[:, place], lse[:, place]
        dots = jnp.sum((grad.astype(F32) * outs[d][...].astype(F32)).T, axis=0, keepdims=True)

        def chunk(at):
            s = attend_chunk(windowed, query, keys, at, mark, kmark)
            p = jnp.exp2(s * (SCALE * LOG2E) - norm_log)
            ds = (p * (dot_t(values[at], grad, 1, 1) - dots)).astype(LOW)
            acc[at, :HD] += dot_t(ds, query)
            acc[at, HD:] += dot_t(p.astype(LOW), grad)
            return dot_t(keys[at], ds, 0, 0)

        if not windowed:
            part = chunk(slice(0, 2 * n))
        else:
            turned[...] = chunk(slice(0, n))
            for e in range(4, 8):

                @pl.when(block_gap(spot, d, e) < 3)
                def _():
                    turned[...] += chunk(slice(TOK * e, TOK * e + TOK))

            part = turned[...]
        dq[d][...] = (part * SCALE).T.astype(LOW)
    for ref, start in ((own, 0), (far, n)):
        ref[:, :HD] = acc[start : start + n, :HD] * SCALE
        ref[:, HD:] = acc[start : start + n, HD:]


def attend_bwd(spot, pieces, grads, mixed, lse, mark, windowed):
    n = 4 * TOK
    old = [windowed] * 8
    outs = [shape((TOK, HD))] * 4 + [shape((n, 2 * HD), F32)] * 2
    *dq, own, far = old_call(
        "attend_bwd",
        functools.partial(bwd_body, windowed),
        outs,
        [pl.BlockSpec(memory_space=pltpu.VMEM)] * 6,
        [*pieces, *grads, *mixed, lse, *mark],
        old + [False] * 4 + old[:4] + [False] * 3,
        [1] * 19,
        spot,
        [pltpu.VMEM((2 * n, HD), LOW)] * 2 + [pltpu.VMEM((2 * n, 2 * HD), F32), pltpu.VMEM((HD, TOK), F32)],
        18,
    )
    return dq, own, far


def join_body(*refs):
    dq, own, far, outs = refs[:4], refs[4], refs[5], refs[6:]
    for d in range(4):
        at = slice(TOK * d, TOK * d + TOK)
        outs[d][:, :HD] = dq[d][...]
        outs[d][:, HD:] = (own[at] + far[at]).astype(LOW)


def join_heads(dq, own, far):
    return call("join_heads", join_body, [shape((TOK, 3 * HD))] * 4, *dq, own, far)


def swap(values, axis, bits, size=4):
    if axis == Y:
        bits = (bits & 1) * 2 + (bits >> 1)
    return lax.ppermute(values, axis, [(i, i ^ bits) for i in range(size)])


def sibling(values):
    return swap(values, "core", 1, 2)


def exchange(pieces, axis):
    got = {d: swap(pieces[d], axis, d) for d in (2, 1, 3)}
    return [pieces[0], got[1], got[2], got[3]]


def gather(piece, axis):
    return exchange([piece] * 4, axis)


def four_sum(parts):
    return (parts[0].astype(F32) + parts[2].astype(F32)) + (parts[1].astype(F32) + parts[3].astype(F32))


def line_sum(values, axis):
    return four_sum(gather(values, axis))


def tie(*values):
    return lax.optimization_barrier(values)


def pick(stacked, index):
    return lax.dynamic_index_in_dim(stacked, index, 0, keepdims=False)


def layer_forward(spot, stream, pieces, matrices, vectors, mark, windowed):
    heads_matrix, up_matrix, down_matrix = matrices
    qkv_bias, up_bias, out_bias, down_bias, attn_gain, attn_shift, ffn_gain, ffn_shift = vectors
    keep, send, *heads = rows_mm("qkv", spot, pieces, heads_matrix, qkv_bias, int(windowed))
    if windowed:
        *heads, heads_matrix = heads
    rows = (keep, send)
    heads = exchange(heads, "x")
    heads = heads + [sibling(h) for h in heads]
    mixed, lse = attend_fwd(spot, heads, mark, windowed)
    *branch, attended = scatter_mm(spot, exchange(mixed, "x"), heads_matrix, 512, 1536)
    normed, scale, first, low = norm(exchange(branch, "z"), stream, out_bias, attn_gain, attn_shift)
    keep, send, active, slope, *loaded = rows_mm("up", spot, gather(low, "z"), up_matrix, up_bias, 2 * windowed)
    if windowed:
        up_matrix, down_matrix = loaded
    second = scatter_mm(spot, [active], down_matrix, 2048, 0)
    normed_two, scale_two, result, low = norm(exchange(second, "z"), first, down_bias, ffn_gain, ffn_shift)
    saved = (heads, mixed, lse, normed, scale, slope, normed_two, scale_two)
    far = [sibling(part) for part in (rows[1], attended, send, active)]
    low, *far = tie(low, *far)
    sides = (rows[0], far[0]), (attended, far[1]), (keep, far[2]), (active, far[3])
    return result, low, saved, sides, (heads_matrix, up_matrix, down_matrix)


FRESH_LEFTS = [False] * 2 + [True] * 6
FRESH_RIGHTS = [True] * 4 + [False] * 2 + [True] * 2


def layer_backward(spot, parts, base, saved, sides, matrices, vectors, mark, windowed, earlier=None, before=(), sums_two=None, turn=None):
    heads_matrix, up_matrix, down_matrix = matrices
    attn_gain, ffn_gain = vectors[4], vectors[6]
    heads, mixed, lse, normed, scale, slope, normed_two, scale_two = saved
    rows, attended, first_rows, active = sides
    last = earlier is not None
    grad_summed, low, ffn_sums = norm_back(parts, base, normed_two, scale_two, ffn_gain)
    keep, send, grad_up, up_sums = rows_mm("slope", spot, gather(low, "z"), down_matrix, slope)
    down_pair = (keep, sibling(send)), active
    up_pair = first_rows, (grad_up, sibling(grad_up))
    if last:
        down_term = weight_term(spot, *two_layers(down_pair, earlier[3]), FRESH_LEFTS)
        grad_up, down_term = tie(grad_up, down_term)
    parts = exchange(scatter_mm(spot, [grad_up], up_matrix, 2048, 0), "z")
    if last:
        down_sum = lax.psum_scatter(down_term, ("ylo", "x"), scatter_dimension=0, tiled=True)
        up_term = weight_term(spot, *two_layers(up_pair, earlier[2]), FRESH_RIGHTS)
    under = (ffn_sums, sums_two[0]) if last else ()
    grad_residual, low, attn_sums = norm_back(parts, grad_summed, normed, scale, attn_gain, under)
    if last:
        low, up_term = tie(low, up_term)
        up_sum = lax.psum_scatter(up_term, ("ylo", "x"), scatter_dimension=0, tiled=True)
    sums = (jnp.concatenate([attn_sums, ffn_sums]), up_sums)
    keep, send, *grad_heads = rows_mm("heads", spot, gather(low, "z"), heads_matrix)
    if last:
        *grad_heads, own_sums = grad_heads
        hidden_sums = by_yhi((up_sums + sums_two[1]).reshape(2, 1024), spot[4])
        sums = jnp.concatenate([own_sums[:6].reshape(24, 512), hidden_sums.reshape(4, 512)])
    out_pair = (keep, sibling(send)), attended
    grad_heads = exchange(grad_heads, "x")
    grad_heads[3], *before = tie(grad_heads[3], *before)
    grad_queries, own_terms, far_terms = attend_bwd(spot, heads, grad_heads, mixed, lse, mark, windowed)
    grad_parts = exchange(join_heads(grad_queries, own_terms, sibling(far_terms)), "x")
    *partial, grad_packed = scatter_mm(spot, grad_parts, heads_matrix, 1536, 0)
    qkv_pair = rows, (grad_packed, sibling(grad_packed))
    if not last:
        return exchange(partial, "z"), grad_residual, (qkv_pair, out_pair, up_pair, down_pair), sums, before
    sides = [*two_layers(qkv_pair, earlier[0]), *two_layers(out_pair, earlier[1])]
    rest, line = head_terms(spot, sides, FRESH_RIGHTS + FRESH_LEFTS)
    rest, line, *partial = tie(rest, line, *partial)
    rest = lax.psum_scatter(rest, "x", scatter_dimension=0, tiled=True)
    low = (four_sum(exchange(partial, "z")) + grad_residual).astype(LOW)
    same, other = turn(low)
    heads = line.reshape(2, 2, 3, 128)
    heads = jnp.stack([by_yhi(heads[j], spot[4]) for j in range(2)]).reshape(3, 512)
    sums = jnp.concatenate([sums, heads, jnp.zeros((1, 512), F32)])
    sums = line_sum(line_sum(sums + sibling(sums), "x"), Y).reshape(-1)
    result = gather(by_micro(spot[4], same, other), "z")
    far = [swap(total[:, 1024:], "yhi", 1, 2) for total in (up_sum, down_sum)]
    rest, *far = tie(rest, *far)
    rest = heads_result(exchange(cut(spot, rest), Y))
    return settle(spot, result), (*rest, *hidden_result(up_sum, far[0], down_sum, far[1])), sums


def two_layers(one, two):
    return list(one[0]) + list(two[0]), list(one[1]) + list(two[1])


def turn_same(core, ylo, values):
    got = lax.ppermute(values, ("core", "ylo"), [(1, 2), (2, 1)])
    return jnp.where(core == ylo, values, got)


def turn_other(values):
    perm = [(c * 4 + l * 2 + h, l * 4 + c * 2 + 1 - h) for c in range(2) for l in range(2) for h in range(2)]
    return lax.ppermute(values, ("core", "ylo", "yhi"), perm)


def by_micro(yhi, same, other):
    return jnp.stack([jnp.where(yhi == 0, same, other), jnp.where(yhi == 0, other, same)])


def by_yhi(values, yhi):
    return jnp.where(yhi == 0, values, values[::-1])


def shards(
    inputs,
    cotangent,
    segments,
    query_weight,
    key_weight,
    value_weight,
    out_weight,
    up_weight,
    down_weight,
    query_bias,
    value_bias,
    out_bias,
    up_bias,
    down_bias,
    attn_gain,
    attn_shift,
    ffn_gain,
    ffn_shift,
):
    core, ylo, x, yhi, z = (lax.axis_index(name) for name in AXES)
    spot = jnp.stack([x, core, ylo, z, yhi]).astype(jnp.int32)
    local = pack_heads(query_weight, key_weight, value_weight, out_weight)
    parts = gather(local, Y)
    *parts, inputs, down_weight = tie(*parts, inputs, down_weight)

    def gathered(heads, parts):
        return lax.all_gather(pair(heads, spot, parts), ("core", "x"), axis=0, tiled=True)

    heads_matrix = gathered(True, parts)
    own_rows = turn_same(core, ylo, pick(pick(inputs, yhi)[0].reshape(4, OWN, D), z))
    pieces = gather(own_rows, "z")
    *pieces, up_weight = tie(*pieces, up_weight)
    hidden_matrix = gathered(False, gather(up_weight, Y) + gather(pack(turn_body, 1024, down_weight), Y))
    matrices = (heads_matrix, hidden_matrix, None)
    bias_own = jnp.concatenate([query_bias, value_bias, up_bias])
    bias = (bias_own, swap(bias_own, "yhi", 1, 2))
    none = jnp.zeros((128,), F32)
    qkv_bias = jnp.concatenate(
        [
            part
            for j in range(2)
            for h in range(2)
            for part in (bias[h][128 * j : 128 * j + 128], none, bias[h][256 + 128 * j : 384 + 128 * j])
        ]
    )
    up_all = jnp.concatenate([bias[h][512:] for h in range(2)])
    vectors = (qkv_bias, up_all, out_bias, down_bias, attn_gain, attn_shift, ffn_gain, ffn_shift)
    vectors = tuple(v[None] for v in vectors)
    top_grad = turn_same(core, ylo, pick(pick(cotangent, yhi)[0].reshape(4, OWN, D), z)).astype(F32)
    seg_here = pick(segments, yhi)[0].astype(F32)
    mark = marks(spot, jnp.where(core == ylo, seg_here, sibling(seg_here)))
    *pieces, mark_row, mark_column = tie(*pieces, *mark)
    mark = (mark_row, mark_column)
    middle, low, saved_one, sides_one, matrices = layer_forward(
        spot, own_rows.astype(F32), pieces, matrices, vectors, mark, True
    )
    _, low, saved_two, sides_two, _ = layer_forward(spot, middle, gather(low, "z"), matrices, vectors, mark, False)
    parts, base, pairs, sums_two, result = layer_backward(
        spot, [], top_grad, saved_two, sides_two, matrices, vectors, mark, False, None, gather(low, "z")
    )
    result = settle(spot, result)
    same, other = turn_same(core, ylo, result), turn_other(result)
    parts[0], same, other = tie(parts[0], same, other)

    def turn(low):
        return turn_same(core, ylo, low), turn_other(low)

    input_grad, matrix_grads, sums = layer_backward(
        spot, parts, base, saved_one, sides_one, matrices, vectors, mark, True, pairs, (), sums_two, turn
    )
    own = sums[: 6 * D].reshape(6, D)
    heads = sums[7 * D : 7 * D + 1536].reshape(2, 2, 3, 128)
    heads = lax.dynamic_index_in_dim(heads, yhi, 1, keepdims=False)
    return (
        by_micro(yhi, same, other)[:, None],
        input_grad[:, None],
        *matrix_grads,
        heads[:, 0].reshape(-1),
        heads[:, 2].reshape(-1),
        own[2],
        pick(sums[6 * D : 7 * D].reshape(2, 1024), yhi),
        own[5],
        own[0],
        own[1],
        own[3],
        own[4],
    )


def solution(mesh):
    split = Mesh(mesh.devices.reshape(2, 2, 4, 2, 4), AXES)
    token = P(None, "core", ("ylo", "x"), None)
    inner = P(("core", "ylo", "x"), ("yhi", "z"))
    outer = P(("yhi", "z"), ("core", "ylo", "x"))
    unit = P(("yhi", "z"))
    matrix = (inner, inner, inner, outer, inner, outer)
    vector = (unit, unit, P(), unit, P(), P(), P(), P(), P())
    in_specs = (token, token, P(None, "core", None)) + matrix + vector
    out_specs = (token, token) + matrix + vector
    return jax.shard_map(shards, mesh=split, in_specs=in_specs, out_specs=out_specs, check_vma=False)
```

```python
import functools

import jax
import jax.numpy as jnp
from jax import lax
from jax.experimental import pallas as pl
from jax.experimental.pallas import tpu as pltpu
from jax.sharding import Mesh, PartitionSpec as P

AXES = ("core", "ylo", "x", "yhi", "z")
Y = ("ylo", "yhi")
ROWS = ("core", "ylo", "x")
D = 2048
HD = 128
TOK = 256
OWN = 64
REACH = 512
LOW = jnp.bfloat16
F32 = jnp.float32
BLOCKED = -1e30
SCALE = HD ** (-0.5)
LOG2E = 1.4426950408889634
EPSILON = 1e-05
CURVE = 0.7978845608028654
CUBIC = 0.044715


def shape(dims, dtype=LOW):
    return jax.ShapeDtypeStruct(dims, dtype)


def dot_t(a, b, ca=1, cb=0):
    return lax.dot_general(a, b, (((ca,), (cb,)), ((), ())), preferred_element_type=F32)


def call(name, body, outs, *args, spot=None, scratch=(), mib=12, flops=0, size=2**21, exps=0):
    specs = [pl.BlockSpec(memory_space=pltpu.VMEM)] * len(args)
    if spot is not None:
        args = (spot,) + args
        specs = [pl.BlockSpec(memory_space=pltpu.SMEM)] + specs
    return pl.pallas_call(
        body,
        in_specs=specs,
        out_specs=[pl.BlockSpec(memory_space=pltpu.VMEM)] * len(outs),
        out_shape=outs,
        scratch_shapes=scratch,
        compiler_params=pltpu.CompilerParams(vmem_limit_bytes=mib * 2**20),
        cost_estimate=pl.CostEstimate(flops=flops, bytes_accessed=size, transcendentals=exps),
        name=name,
    )(*args)


def at_block(index, size):
    return pl.ds(pl.multiple_of(index * size, size), size)


def pack_heads_body(q_far, k_far, v_far, o_far, out, q, k, v, o, sems):
    copies = [
        pltpu.make_async_copy(far, part, sems.at[i])
        for i, (far, part) in enumerate(((q_far, q), (k_far, k), (v_far, v), (o_far, o)))
    ]
    for copy in copies:
        copy.start()
    for copy in copies:
        copy.wait()
    for j in range(2):
        at = slice(128 * j, 128 * j + 128)
        for t, part in enumerate((q, k, v)):
            out[:, 384 * j + 128 * t : 384 * j + 128 * t + 128] = part[:, at]
    out[:, 768:] = o[...].T


def pack_heads(*parts):
    return pl.pallas_call(
        pack_heads_body,
        in_specs=[pl.BlockSpec(memory_space=pl.ANY)] * 4,
        out_specs=pl.BlockSpec(memory_space=pltpu.VMEM),
        out_shape=shape((128, 1024)),
        scratch_shapes=[pltpu.VMEM(part.shape, part.dtype) for part in parts] + [pltpu.SemaphoreType.DMA((4,))],
        compiler_params=pltpu.CompilerParams(vmem_limit_bytes=2**22),
        cost_estimate=pl.CostEstimate(flops=0, bytes_accessed=2**19, transcendentals=0),
        name="pack_heads",
    )(*[pltpu.with_memory_space_constraint(part, pltpu.HBM) for part in parts])


def turn_body(down, out):
    out[...] = down[...].T


def join_heads_columns(own, far, out, rows):
    for j in range(2):
        for h, part in enumerate((own, far)):
            slot = 2 * j + h
            out[rows, 384 * slot : 384 * slot + 384] = part[:, 384 * j : 384 * j + 384]
            out[rows, 1536 + 128 * slot : 1664 + 128 * slot] = part[:, 768 + 128 * j : 896 + 128 * j]


def pair_body(heads, spot, *refs):
    parts, out = refs[:-1], refs[-1]
    for ylo in range(2):
        rows = at_block(ylo ^ spot[2], 128)
        if heads:
            join_heads_columns(parts[ylo], parts[ylo + 2], out, rows)
            continue
        for i, d in enumerate((ylo, ylo + 2, ylo + 4, ylo + 6)):
            out[rows, 1024 * i : 1024 * i + 1024] = parts[d][...]


def pair(heads, spot, parts):
    outs = [shape((256, 2048 if heads else 4096))]
    return call("pair", functools.partial(pair_body, heads), outs, *parts, spot=spot)[0]


def pack(body, width, *parts):
    return call("pack", body, [shape((128, width))], *parts)[0]


def turned_rows(source, kept, columns, to, sems):
    copies = []
    for core in range(2):
        for ylo in range(2):
            for x in range(4):
                at, row = 256 * (4 * core + x) + 128 * ylo, 1024 * core + 512 * ylo + 128 * x
                part = source.at[pl.ds(at, 128), pl.ds(columns[0], columns[1])]
                place = kept.at[pl.ds(row, 128), pl.ds(to, columns[1])]
                copies.append(pltpu.make_async_copy(part, place, sems.at[len(copies)]))
    return copies


def held(matrix):
    return pltpu.with_memory_space_constraint(matrix, pltpu.VMEM)


def settle_body(spot, p0, p1, p2, p3, out):
    for d, part in enumerate((p0, p1, p2, p3)):
        at = at_block(d ^ spot[3], OWN)
        if len(out.shape) == 2:
            out[at] = part[...]
        else:
            out[:, at] = part[...]


def settle(spot, parts):
    return call("settle", settle_body, [shape(parts[0].shape[:-2] + (TOK, D))], *parts, spot=spot)[0]


def four(refs, at):
    p = [ref[at].astype(F32) for ref in refs]
    return (p[0] + p[2]) + (p[1] + p[3])


def rows_body(kind, first, loads, spot, p0, p1, p2, p3, w, *refs):
    extra = refs[0] if kind != "heads" else None
    keep, send, *outs = refs[1:] if kind != "heads" else refs
    chunks, later = [], []
    if loads:
        source = w
        *outs, sems = outs
        w, *more = outs[-loads:]
        outs = outs[:-loads]
        chunks = [turned_rows(source, w, (512 * c, 512), 512 * c, sems.at[c]) for c in range(4)]
        later = [turned_rows(source, ref, (2048, 2048), 0, sems.at[4]) for ref in more]
        for chunk in chunks + later:
            for copy in chunk:
                copy.start()

    def loaded(count):
        while chunks and 4 - len(chunks) < count:
            for copy in chunks.pop(0):
                copy.wait()

    kept, sent = at_block(spot[1], D // 2), at_block(1 - spot[1], D // 2)
    for i, p in enumerate((p0, p1, p2, p3)):
        keep[OWN * i : OWN * i + OWN] = p[:OWN, kept]
        send[OWN * i : OWN * i + OWN] = p[:OWN, sent]
    if p0.shape[0] > OWN:
        *outs, sums = outs
        sums[...] = four((p0, p1, p2, p3), slice(OWN, OWN + 16))

    def product(at):
        return dot_t(keep[...], w[kept, at]) + dot_t(send[...], w[sent, at])

    if kind == "qkv" and loads:
        for slot in range(4):
            loaded(slot if slot else 1)
            low = (product(slice(384 * slot, 384 * slot + 384)) + extra[:, 384 * slot : 384 * slot + 384]).astype(LOW)
            for d in range(4):

                @pl.when((slot ^ spot[0]) == d)
                def _():
                    outs[d][...] = low

        loaded(4)
        return
    if kind in ("qkv", "heads"):
        width = outs[0].shape[1]
        for d in range(4):
            slot = d ^ spot[0]
            values = product(pl.ds(pl.multiple_of(first + slot * width, 128), width))
            if kind == "qkv":
                values = values + extra[:, at_block(slot, width)]
            outs[d][...] = values.astype(LOW)
        return
    tile = 512
    for i in range(4):
        at = slice(tile * i, tile * i + tile)
        loaded(i + 1)
        values = product(at)
        if kind == "up":
            values = values + extra[:, at]
            square = values * values
            bend = jnp.tanh(CURVE * (values + CUBIC * (square * values)))
            outs[0][:, at] = (0.5 * values * (1.0 + bend)).astype(LOW)
            slope = 0.5 * (1.0 + bend) + 0.5 * values * (1.0 - bend * bend) * (CURVE * (1.0 + 3.0 * CUBIC * square))
            outs[1][:, at] = slope.astype(LOW)
        else:
            low = (values * extra[:, at].astype(F32)).astype(LOW)
            outs[0][:, at] = low
            outs[1][:, at] = jnp.sum(low.astype(F32), axis=0, keepdims=True)
    for chunk in later:
        for copy in chunk:
            copy.wait()


def rows_mm(kind, spot, pieces, weight, extra=None, loads=0):
    half = shape((TOK, D // 2))
    n, first, outs = {
        "qkv": (1536, 0, [shape((TOK, 384))] * 4),
        "heads": (512, 1536, [shape((TOK, HD))] * 4),
        "up": (2048, 0, [shape((TOK, 2048))] * 2),
        "slope": (2048, 0, [shape((TOK, 2048)), shape((1, 2048), F32)]),
    }[kind]
    args = [weight if loads else held(weight)] + ([] if extra is None else [extra])
    if pieces[0].shape[0] > OWN:
        outs = [*outs, shape((16, D), F32)]
    body = functools.partial(rows_body, kind, first, loads)
    cost = pl.CostEstimate(flops=2 * TOK * D * n, bytes_accessed=2 * D * n, transcendentals=TOK * n if kind == "up" else 0)
    vmem = pl.BlockSpec(memory_space=pltpu.VMEM)
    if loads:
        args[0] = pltpu.with_memory_space_constraint(weight, pltpu.HBM)
    return pl.pallas_call(
        body,
        in_specs=[pl.BlockSpec(memory_space=pltpu.SMEM)]
        + [vmem] * 4
        + [pl.BlockSpec(memory_space=pl.ANY) if loads else vmem]
        + [vmem] * (len(args) - 1),
        out_specs=[vmem] * (2 + len(outs) + loads),
        out_shape=[half, half, *outs] + [pltpu.VMEM((D, 2048), LOW)] * loads,
        scratch_shapes=[pltpu.SemaphoreType.DMA((5, 16))] if loads else [],
        compiler_params=pltpu.CompilerParams(vmem_limit_bytes=12 * 2**20),
        cost_estimate=cost,
        name="rows_" + kind,
    )(spot, *pieces, *args)


def scatter_body(n_parts, first, k, spot, *refs):
    parts, w, outs = refs[:n_parts], refs[n_parts], refs[n_parts + 1 : n_parts + 5]
    if n_parts == 1:
        rows = parts[0]
    else:
        rows = refs[n_parts + 5]
        for d, part in enumerate(parts):
            rows[:, at_block(d ^ spot[0], k // 4)] = part[...]
    tile = 512
    for i in range(D // tile):
        to = slice(tile * i, tile * i + tile)
        values = dot_t(rows[...], w[to, first : first + k], 1, 1)
        outs[0][:, to] = values[:OWN]
        for d in range(1, 4):
            outs[d][:, to] = values[OWN * d : OWN * d + OWN].astype(LOW)


def scatter_mm(spot, parts, weight, k, first):
    outs = [shape((OWN, D), F32)] + [shape((OWN, D))] * 3
    if len(parts) > 1:
        outs.append(shape((TOK, k)))
    return call(
        "scatter_mm",
        functools.partial(scatter_body, len(parts), first, k),
        outs,
        *parts,
        held(weight),
        spot=spot,
        flops=2 * TOK * D * k,
        size=2 * D * k,
    )


def fetched(refs, olds, buffers, sems, chunks):
    ready, copies, at = [], [], 0
    for ref, old, count in zip(refs, olds, chunks):
        if not old:
            ready.append(ref)
            copies.append([None] * count)
            continue
        n = ref.shape[1] // count
        parts = [(pl.ds(0, ref.shape[0]), pl.ds(n * c, n)) for c in range(count)]
        ready.append(buffers[at])
        copies.append([pltpu.make_async_copy(ref.at[p], buffers[at].at[p], sems.at[at, c]) for c, p in enumerate(parts)])
        at += 1
    for c in range(max(chunks)):
        for mine in copies:
            if c < len(mine) and mine[c] is not None:
                mine[c].start()
    return ready, copies


def arrive(copies):
    for copy in copies:
        if copy is not None:
            copy.wait()


def old_call(name, body, outs, out_specs, operands, olds, chunks, spot, scratch, mib):
    buffers = [pltpu.VMEM(a.shape, a.dtype) for a, old in zip(operands, olds) if old]
    n_in, n_old = len(operands), len(buffers)

    def inner(spot_ref, *refs):
        out_refs = refs[n_in : n_in + len(outs)]
        rest = refs[n_in + len(outs) :]
        ready, copies = fetched(refs[:n_in], olds, rest[:n_old], rest[n_old], chunks)
        body(spot_ref, ready, copies, out_refs, rest[n_old + 1 :])

    args = [pltpu.with_memory_space_constraint(a, pltpu.HBM) if old else a for a, old in zip(operands, olds)]
    return pl.pallas_call(
        inner,
        in_specs=[pl.BlockSpec(memory_space=pltpu.SMEM)]
        + [pl.BlockSpec(memory_space=pl.ANY if old else pltpu.VMEM) for old in olds],
        out_specs=out_specs,
        out_shape=outs,
        scratch_shapes=[*buffers, pltpu.SemaphoreType.DMA((max(n_old, 1), max(chunks))), *scratch],
        compiler_params=pltpu.CompilerParams(vmem_limit_bytes=mib * 2**20),
        cost_estimate=pl.CostEstimate(flops=2**32, bytes_accessed=2**23, transcendentals=0),
        name=name,
    )(spot, *args)


def term_body(spot, operands, copies, outs, scratch):
    turned, parts, sems = scratch
    for i in range(4):
        arrive(copies[i])
        turned[:, TOK * i : TOK * i + TOK] = operands[i][...].T
    sent = []
    for step in range(4):
        at = slice(512 * step, 512 * step + 512)
        arrive([copies[4 + i][step] for i in range(4)])
        total = None
        for i in range(4):
            part = dot_t(turned[:, TOK * i : TOK * i + TOK], operands[4 + i][:, at])
            total = part if total is None else total + part
        if step > 1:
            sent[step - 2].wait()
        parts[step & 1] = total.astype(LOW)
        sent.append(pltpu.make_async_copy(parts.at[step & 1], outs[0].at[:, pl.ds(512 * step, 512)], sems.at[step & 1]))
        sent[-1].start()
    arrive(sent[2:])


def weight_term(spot, lefts, rights, olds):
    return old_call(
        "weight_term",
        term_body,
        [pltpu.HBM((1024, 2048), LOW)],
        [pl.BlockSpec(memory_space=pl.ANY)],
        [*lefts, *rights],
        olds,
        [1] * 4 + [4] * 4,
        spot,
        [pltpu.VMEM((1024, 1024), LOW), pltpu.VMEM((2, 1024, 512), LOW), pltpu.SemaphoreType.DMA((2,))],
        16,
    )[0]


def head_terms_body(spot, operands, copies, outs, scratch):
    *turned, parts, sems = scratch
    rights = operands[4:8], operands[12:16]
    for g in range(2):
        for i in range(4):
            arrive(copies[8 * g + i])
            for x in range(4):
                for ylo in range(2):
                    at, to = 512 * ylo + 128 * x, 256 * x + 128 * ylo
                    turned[g][to : to + 128, TOK * i : TOK * i + TOK] = operands[8 * g + i][:, at : at + 128].T
    for i in (*range(4, 8), *range(12, 16)):
        arrive(copies[i])
    sent = []
    for slot in range(4):
        if slot > 1:
            arrive(sent[2 * slot - 4 : 2 * slot - 2])
        first = 1024 * (slot & 1)
        at = 0
        for g, width in enumerate((384, 128)):
            total = None
            for i in range(4):
                part = dot_t(turned[g][:, TOK * i : TOK * i + TOK], rights[g][i][:, width * slot : width * slot + width])
                total = part if total is None else total + part
            held_part = parts.at[slot & 1, :, pl.ds(at, width)]
            held_part[...] = total.astype(LOW)
            to = first + width * (slot >> 1)
            sent.append(pltpu.make_async_copy(held_part, outs[0].at[:, pl.ds(to, width)], sems.at[slot & 1, g]))
            sent[-1].start()
            first += 2 * width
            at += width
    line = [jnp.sum(rights[0][i][...].astype(F32), axis=0, keepdims=True) for i in (0, 2)]
    outs[1][...] = line[0] + line[1]
    arrive(sent[4:])


def head_terms(spot, sides, olds):
    return old_call(
        "head_terms",
        head_terms_body,
        [pltpu.HBM((1024, 2048), LOW), shape((1, 1536), F32)],
        [pl.BlockSpec(memory_space=pl.ANY), pl.BlockSpec(memory_space=pltpu.VMEM)],
        [part for side in sides for part in side],
        olds,
        [1] * 16,
        spot,
        [pltpu.VMEM((1024, 1024), LOW)] * 2 + [pltpu.VMEM((2, 1024, 512), LOW), pltpu.SemaphoreType.DMA((2, 2))],
        20,
    )


def cut_body(spot, total, *outs):
    for d in range(4):
        outs[d][...] = total[at_block((d & 1) ^ spot[2], 128), 1024 * (d >> 1) : 1024 * (d >> 1) + 1024]


def cut(spot, total):
    return call("cut", cut_body, [shape((128, 1024))] * 4, total, spot=spot)


def heads_result_body(p0, p1, p2, p3, q, k, v, o):
    total = four((p0, p1, p2, p3), slice(None))
    for j in range(2):
        to = slice(128 * j, 128 * j + 128)
        for t, ref in enumerate((q, k, v)):
            at = 384 * j + 128 * t
            ref[:, to] = total[:, at : at + 128]
        o[to] = total[:, 768 + 128 * j : 896 + 128 * j].T


def heads_result(parts):
    square = shape((128, 256), F32)
    return call("heads_result", heads_result_body, [square, square, square, shape((256, 128), F32)], *parts)


def far_body(up, down, out):
    out[:128] = up[:, 1024:]
    out[128:] = down[:, 1024:]


def far_halves(up, down):
    return call("far_halves", far_body, [shape((256, 1024))], up, down)[0]


def hidden_result_body(up, down, far, up_out, down_out):
    up_out[...] = up[:, :1024].astype(F32) + far[:128].astype(F32)
    down_out[...] = (down[:, :1024].astype(F32) + far[128:].astype(F32)).T


def hidden_result(*parts):
    return call("hidden_result", hidden_result_body, [shape((128, 1024), F32), shape((1024, 128), F32)], *parts)


def norm_body(given, *refs):
    parts, (base, bias, gain, shift, normed, scale, result, low) = refs[:given], refs[given:]
    values = base[...] + bias[...] + ((parts[0][...] + parts[2][...].astype(F32)) + (parts[1][...].astype(F32) + parts[3][...].astype(F32)))
    center = jnp.mean(values, axis=-1, keepdims=True)
    centered = values - center
    spread = jnp.mean(centered * centered, axis=-1, keepdims=True)
    root = lax.rsqrt(spread + EPSILON)
    unit = centered * root
    normed[...] = unit
    scale[...] = root
    values = unit * gain[...] + shift[...]
    result[...] = values
    low[...] = values.astype(LOW)


def norm(parts, base, bias, gain, shift):
    rows = shape((OWN, D), F32)
    outs = [rows, shape((OWN, 1), F32), rows, shape((OWN, D))]
    return call("norm", functools.partial(norm_body, 4), outs, *parts, base, bias, gain, shift, flops=2**21)


def norm_back_body(given, under, *refs):
    parts, (base, normed, scale, gain, *refs) = refs[:given], refs[given:]
    if under:
        ffn_sums, sums_two, *refs = refs
    back, low, sums = refs
    grad = base[...]
    if given:
        grad = grad + ((parts[0][...] + parts[2][...].astype(F32)) + (parts[1][...].astype(F32) + parts[3][...].astype(F32)))
    unit = normed[...]
    tilted = grad * gain[...]
    values = tilted - jnp.mean(tilted, axis=-1, keepdims=True) - unit * jnp.mean(tilted * unit, axis=-1, keepdims=True)
    values = values * scale[...]
    back[...] = values
    cut = values.astype(LOW)
    low[:OWN] = cut
    lines = [jnp.sum(part, axis=0, keepdims=True) for part in (grad * unit, grad, cut.astype(F32))]
    for i, line in enumerate(lines):
        sums[i : i + 1] = line
    if under:
        lines = jnp.concatenate([*lines, ffn_sums[...], jnp.zeros((10, D), F32)], axis=0)
        both = jnp.concatenate([sums_two[...], jnp.zeros((10, D), F32)], axis=0)
        low[OWN:] = (lines + both).astype(LOW)


def norm_back(parts, base, normed, scale, gain, under=()):
    outs = [shape((OWN, D), F32), shape((OWN + 16 * bool(under), D)), shape((3, D), F32)]
    body = functools.partial(norm_back_body, len(parts), bool(under))
    return call("norm_back", body, outs, *parts, base, normed, scale, gain, *under, flops=2**21)


def marks_body(spot, seg, row, column, table):
    lane = lax.broadcasted_iota(jnp.int32, (1, 64), 1)
    for i in range(32):
        block = ((spot[1] ^ (i >> 4)) * 4 + (spot[0] ^ ((i >> 2) & 3))) * 4 + (spot[3] ^ (i & 3))
        line = seg[pl.ds(block, 1)] * 8192.0 + (block * 64 + lane).astype(F32)
        table[i : i + 1] = line
        if i < 16:
            row[:, 64 * i : 64 * i + 64] = line
    turned = table[...].T
    for i in range(32):
        column[64 * i : 64 * i + 64] = turned[:, i : i + 1]


def marks(spot, seg):
    outs = [shape((1, 1024), F32), shape((2048, 1), F32)]
    return call("marks", marks_body, outs, seg.reshape(32, 64), spot=spot, scratch=[pltpu.VMEM((32, 64), F32)])


def near(marks, keys, windowed):
    return jnp.abs(marks - keys) <= (REACH if windowed else 2047.0)


def load_heads(pieces, keys, values):
    for i, piece in enumerate(pieces):
        at = slice(TOK * i, TOK * i + TOK)
        keys[at] = piece[:, HD : 2 * HD]
        values[at] = piece[:, 2 * HD :]


def block_gap(spot, d, e):
    query, key = spot[0] ^ d, spot[0] ^ (e & 3)
    gap = jnp.abs(query - key)
    if e < 4:
        return gap
    return jnp.where(spot[1] == 0, 4 + key - query, 4 + query - key)


def attend_chunk(windowed, query, keys, at, qmark, kmark):
    s = dot_t(keys[at], query, 1, 1)
    return jnp.where(near(qmark, kmark[at], windowed), s, BLOCKED)


def fwd_body(windowed, spot, *refs):
    pieces, qmark, kmark = refs[:8], refs[8], refs[9]
    outs, lse, keys, values, best, total, mixed = refs[10:14], *refs[14:]
    load_heads(pieces, keys, values)
    own = slice(0, 4 * TOK if windowed else 8 * TOK)
    for d in range(4):
        at = slice(TOK * d, TOK * d + TOK)
        query, mark = pieces[d][:, :HD], qmark[:, at]
        s = attend_chunk(windowed, query, keys, own, mark, kmark)
        top = jnp.max(s, axis=0, keepdims=True)
        p = jnp.exp2((s - top) * (SCALE * LOG2E))
        count = jnp.sum(p, axis=0, keepdims=True)
        part = dot_t(values[own], p.astype(LOW), 0, 0)
        if windowed:
            best[...], total[...], mixed[...] = top, count, part
            for e in range(4, 8):

                @pl.when(block_gap(spot, d, e) < 3)
                def _():
                    far = slice(TOK * e, TOK * e + TOK)
                    s = attend_chunk(windowed, query, keys, far, mark, kmark)
                    top = jnp.maximum(best[...], jnp.max(s, axis=0, keepdims=True))
                    p = jnp.exp2((s - top) * (SCALE * LOG2E))
                    less = jnp.exp2((best[...] - top) * (SCALE * LOG2E))
                    total[...] = total[...] * less + jnp.sum(p, axis=0, keepdims=True)
                    mixed[...] = mixed[...] * less + dot_t(values[far], p.astype(LOW), 0, 0)
                    best[...] = top

            top, count, part = best[...], total[...], mixed[...]
        outs[d][...] = (part / count).T.astype(LOW)
        lse[:, at] = top * (SCALE * LOG2E) + jnp.log2(count)


def attend_fwd(spot, pieces, mark, windowed):
    n = 4 * TOK
    *mixed, lse = call(
        "attend_fwd",
        functools.partial(fwd_body, windowed),
        [shape((TOK, HD))] * 4 + [shape((1, n), F32)],
        *pieces,
        *mark,
        spot=spot,
        scratch=[pltpu.VMEM((2 * n, HD), LOW)] * 2
        + [pltpu.VMEM((1, TOK), F32)] * 2
        + [pltpu.VMEM((HD, TOK), F32)],
        mib=12,
        flops=8 * n * n * HD,
        size=2**22,
        exps=2 * n * n,
    )
    return mixed, lse


def bwd_body(windowed, spot, refs, copies, results, scratch):
    pieces, grads, outs, lse, qmark, kmark = refs[:8], refs[8:12], refs[12:16], *refs[16:]
    (*dq, own, far), (keys, values, acc, turned) = results, scratch
    n = 4 * TOK
    for copy in copies:
        arrive(copy)
    load_heads(pieces, keys, values)
    acc[...] = jnp.zeros_like(acc)
    for d in range(4):
        place = slice(TOK * d, TOK * d + TOK)
        query, grad, mark, norm_log = pieces[d][:, :HD], grads[d][...], qmark[:, place], lse[:, place]
        dots = jnp.sum((grad.astype(F32) * outs[d][...].astype(F32)).T, axis=0, keepdims=True)

        def chunk(at):
            s = attend_chunk(windowed, query, keys, at, mark, kmark)
            p = jnp.exp2(s * (SCALE * LOG2E) - norm_log)
            ds = (p * (dot_t(values[at], grad, 1, 1) - dots)).astype(LOW)
            acc[at, :HD] += dot_t(ds, query)
            acc[at, HD:] += dot_t(p.astype(LOW), grad)
            return dot_t(keys[at], ds, 0, 0)

        if not windowed:
            part = chunk(slice(0, 2 * n))
        else:
            turned[...] = chunk(slice(0, n))
            for e in range(4, 8):

                @pl.when(block_gap(spot, d, e) < 3)
                def _():
                    turned[...] += chunk(slice(TOK * e, TOK * e + TOK))

            part = turned[...]
        dq[d][...] = (part * SCALE).T.astype(LOW)
    for ref, start in ((own, 0), (far, n)):
        ref[:, :HD] = acc[start : start + n, :HD] * SCALE
        ref[:, HD:] = acc[start : start + n, HD:]


def attend_bwd(spot, pieces, grads, mixed, lse, mark, windowed):
    n = 4 * TOK
    old = [windowed] * 8
    outs = [shape((TOK, HD))] * 4 + [shape((n, 2 * HD), F32)] * 2
    *dq, own, far = old_call(
        "attend_bwd",
        functools.partial(bwd_body, windowed),
        outs,
        [pl.BlockSpec(memory_space=pltpu.VMEM)] * 6,
        [*pieces, *grads, *mixed, lse, *mark],
        old + [False] * 4 + old[:4] + [False] * 3,
        [1] * 19,
        spot,
        [pltpu.VMEM((2 * n, HD), LOW)] * 2 + [pltpu.VMEM((2 * n, 2 * HD), F32), pltpu.VMEM((HD, TOK), F32)],
        18,
    )
    return dq, own, far


def join_body(*refs):
    dq, own, far, outs = refs[:4], refs[4], refs[5], refs[6:]
    for d in range(4):
        at = slice(TOK * d, TOK * d + TOK)
        outs[d][:, :HD] = dq[d][...]
        outs[d][:, HD:] = (own[at] + far[at]).astype(LOW)


def join_heads(dq, own, far):
    return call("join_heads", join_body, [shape((TOK, 3 * HD))] * 4, *dq, own, far)


def swap(values, axis, bits, size=4):
    if axis == Y:
        bits = (bits & 1) * 2 + (bits >> 1)
    return lax.ppermute(values, axis, [(i, i ^ bits) for i in range(size)])


def sibling(values):
    return swap(values, "core", 1, 2)


def exchange(pieces, axis):
    got = {d: swap(pieces[d], axis, d) for d in (2, 1, 3)}
    return [pieces[0], got[1], got[2], got[3]]


def gather(piece, axis):
    return exchange([piece] * 4, axis)


def four_sum(parts):
    return (parts[0].astype(F32) + parts[2].astype(F32)) + (parts[1].astype(F32) + parts[3].astype(F32))


def line_sum(values, axis):
    return four_sum(gather(values, axis))


def tie(*values):
    return lax.optimization_barrier(values)


def pick(stacked, index):
    return lax.dynamic_index_in_dim(stacked, index, 0, keepdims=False)


def layer_forward(spot, stream, pieces, matrices, vectors, mark, windowed):
    heads_matrix, up_matrix, down_matrix = matrices
    qkv_bias, up_bias, out_bias, down_bias, attn_gain, attn_shift, ffn_gain, ffn_shift = vectors
    keep, send, *heads = rows_mm("qkv", spot, pieces, heads_matrix, qkv_bias, int(windowed))
    if windowed:
        *heads, heads_matrix = heads
    rows = (keep, send)
    heads = exchange(heads, "x")
    heads = heads + [sibling(h) for h in heads]
    mixed, lse = attend_fwd(spot, heads, mark, windowed)
    *branch, attended = scatter_mm(spot, exchange(mixed, "x"), heads_matrix, 512, 1536)
    normed, scale, first, low = norm(exchange(branch, "z"), stream, out_bias, attn_gain, attn_shift)
    keep, send, active, slope, *loaded = rows_mm("up", spot, gather(low, "z"), up_matrix, up_bias, 2 * windowed)
    if windowed:
        up_matrix, down_matrix = loaded
    second = scatter_mm(spot, [active], down_matrix, 2048, 0)
    normed_two, scale_two, result, low = norm(exchange(second, "z"), first, down_bias, ffn_gain, ffn_shift)
    saved = (heads, mixed, lse, normed, scale, slope, normed_two, scale_two)
    far = [sibling(part) for part in (rows[1], attended, send, active)]
    low, *far = tie(low, *far)
    sides = (rows[0], far[0]), (attended, far[1]), (keep, far[2]), (active, far[3])
    return result, low, saved, sides, (heads_matrix, up_matrix, down_matrix)


FRESH_LEFTS = [False] * 2 + [True] * 6
FRESH_RIGHTS = [True] * 4 + [False] * 2 + [True] * 2


def layer_backward(spot, parts, base, saved, sides, matrices, vectors, mark, windowed, earlier=None, before=(), sums_two=None, turn=None):
    heads_matrix, up_matrix, down_matrix = matrices
    attn_gain, ffn_gain = vectors[4], vectors[6]
    heads, mixed, lse, normed, scale, slope, normed_two, scale_two = saved
    rows, attended, first_rows, active = sides
    last = earlier is not None
    grad_summed, low, ffn_sums = norm_back(parts, base, normed_two, scale_two, ffn_gain)
    keep, send, grad_up, up_sums = rows_mm("slope", spot, gather(low, "z"), down_matrix, slope)
    down_pair = (keep, sibling(send)), active
    up_pair = first_rows, (grad_up, sibling(grad_up))
    if last:
        down_term = weight_term(spot, *two_layers(down_pair, earlier[3]), FRESH_LEFTS)
        grad_up, down_term = tie(grad_up, down_term)
    parts = exchange(scatter_mm(spot, [grad_up], up_matrix, 2048, 0), "z")
    if last:
        down_sum = lax.psum_scatter(down_term, ("ylo", "x"), scatter_dimension=0, tiled=True)
        up_term = weight_term(spot, *two_layers(up_pair, earlier[2]), FRESH_RIGHTS)
    under = (ffn_sums, sums_two[0]) if last else ()
    grad_residual, low, attn_sums = norm_back(parts, grad_summed, normed, scale, attn_gain, under)
    if last:
        low, up_term = tie(low, up_term)
        up_sum = lax.psum_scatter(up_term, ("ylo", "x"), scatter_dimension=0, tiled=True)
    sums = (jnp.concatenate([attn_sums, ffn_sums]), up_sums)
    keep, send, *grad_heads = rows_mm("heads", spot, gather(low, "z"), heads_matrix)
    if last:
        *grad_heads, own_sums = grad_heads
        hidden_sums = by_yhi((up_sums + sums_two[1]).reshape(2, 1024), spot[4])
        sums = jnp.concatenate([own_sums[:6].reshape(24, 512), hidden_sums.reshape(4, 512)])
    out_pair = (keep, sibling(send)), attended
    grad_heads = exchange(grad_heads, "x")
    grad_heads[3], *before = tie(grad_heads[3], *before)
    grad_queries, own_terms, far_terms = attend_bwd(spot, heads, grad_heads, mixed, lse, mark, windowed)
    grad_parts = exchange(join_heads(grad_queries, own_terms, sibling(far_terms)), "x")
    *partial, grad_packed = scatter_mm(spot, grad_parts, heads_matrix, 1536, 0)
    qkv_pair = rows, (grad_packed, sibling(grad_packed))
    if not last:
        return exchange(partial, "z"), grad_residual, (qkv_pair, out_pair, up_pair, down_pair), sums, before
    sides = [*two_layers(qkv_pair, earlier[0]), *two_layers(out_pair, earlier[1])]
    rest, line = head_terms(spot, sides, FRESH_RIGHTS + FRESH_LEFTS)
    rest, line, *partial = tie(rest, line, *partial)
    rest = lax.psum_scatter(rest, "x", scatter_dimension=0, tiled=True)
    low = (four_sum(exchange(partial, "z")) + grad_residual).astype(LOW)
    same, other = turn(low)
    heads = line.reshape(2, 2, 3, 128)
    heads = jnp.stack([by_yhi(heads[j], spot[4]) for j in range(2)]).reshape(3, 512)
    sums = jnp.concatenate([sums, heads, jnp.zeros((1, 512), F32)])
    sums = line_sum(line_sum(sums + sibling(sums), "x"), Y).reshape(-1)
    result = gather(by_micro(spot[4], same, other), "z")
    far = swap(far_halves(up_sum, down_sum), "yhi", 1, 2)
    rest, far = tie(rest, far)
    rest = heads_result(exchange(cut(spot, rest), Y))
    return settle(spot, result), (*rest, *hidden_result(up_sum, down_sum, far)), sums


def two_layers(one, two):
    return list(one[0]) + list(two[0]), list(one[1]) + list(two[1])


def turn_same(core, ylo, values):
    got = lax.ppermute(values, ("core", "ylo"), [(1, 2), (2, 1)])
    return jnp.where(core == ylo, values, got)


def turn_other(values):
    perm = [(c * 4 + l * 2 + h, l * 4 + c * 2 + 1 - h) for c in range(2) for l in range(2) for h in range(2)]
    return lax.ppermute(values, ("core", "ylo", "yhi"), perm)


def by_micro(yhi, same, other):
    return jnp.stack([jnp.where(yhi == 0, same, other), jnp.where(yhi == 0, other, same)])


def by_yhi(values, yhi):
    return jnp.where(yhi == 0, values, values[::-1])


def shards(
    inputs,
    cotangent,
    segments,
    query_weight,
    key_weight,
    value_weight,
    out_weight,
    up_weight,
    down_weight,
    query_bias,
    value_bias,
    out_bias,
    up_bias,
    down_bias,
    attn_gain,
    attn_shift,
    ffn_gain,
    ffn_shift,
):
    core, ylo, x, yhi, z = (lax.axis_index(name) for name in AXES)
    spot = jnp.stack([x, core, ylo, z, yhi]).astype(jnp.int32)
    local = pack_heads(query_weight, key_weight, value_weight, out_weight)
    parts = gather(local, Y)
    *parts, inputs, down_weight = tie(*parts, inputs, down_weight)

    def gathered(heads, parts):
        return lax.all_gather(pair(heads, spot, parts), ("core", "x"), axis=0, tiled=True)

    heads_matrix = gathered(True, parts)
    own_rows = turn_same(core, ylo, pick(pick(inputs, yhi)[0].reshape(4, OWN, D), z))
    pieces = gather(own_rows, "z")
    *pieces, up_weight = tie(*pieces, up_weight)
    hidden_matrix = gathered(False, gather(up_weight, Y) + gather(pack(turn_body, 1024, down_weight), Y))
    matrices = (heads_matrix, hidden_matrix, None)
    bias_own = jnp.concatenate([query_bias, value_bias, up_bias])
    bias = (bias_own, swap(bias_own, "yhi", 1, 2))
    none = jnp.zeros((128,), F32)
    qkv_bias = jnp.concatenate(
        [
            part
            for j in range(2)
            for h in range(2)
            for part in (bias[h][128 * j : 128 * j + 128], none, bias[h][256 + 128 * j : 384 + 128 * j])
        ]
    )
    up_all = jnp.concatenate([bias[h][512:] for h in range(2)])
    vectors = (qkv_bias, up_all, out_bias, down_bias, attn_gain, attn_shift, ffn_gain, ffn_shift)
    vectors = tuple(v[None] for v in vectors)
    top_grad = turn_same(core, ylo, pick(pick(cotangent, yhi)[0].reshape(4, OWN, D), z)).astype(F32)
    seg_here = pick(segments, yhi)[0].astype(F32)
    mark = marks(spot, jnp.where(core == ylo, seg_here, sibling(seg_here)))
    *pieces, mark_row, mark_column = tie(*pieces, *mark)
    mark = (mark_row, mark_column)
    middle, low, saved_one, sides_one, matrices = layer_forward(
        spot, own_rows.astype(F32), pieces, matrices, vectors, mark, True
    )
    _, low, saved_two, sides_two, _ = layer_forward(spot, middle, gather(low, "z"), matrices, vectors, mark, False)
    parts, base, pairs, sums_two, result = layer_backward(
        spot, [], top_grad, saved_two, sides_two, matrices, vectors, mark, False, None, gather(low, "z")
    )
    result = settle(spot, result)
    same, other = turn_same(core, ylo, result), turn_other(result)
    parts[0], same, other = tie(parts[0], same, other)

    def turn(low):
        return turn_same(core, ylo, low), turn_other(low)

    input_grad, matrix_grads, sums = layer_backward(
        spot, parts, base, saved_one, sides_one, matrices, vectors, mark, True, pairs, (), sums_two, turn
    )
    own = sums[: 6 * D].reshape(6, D)
    heads = sums[7 * D : 7 * D + 1536].reshape(2, 2, 3, 128)
    heads = lax.dynamic_index_in_dim(heads, yhi, 1, keepdims=False)
    return (
        by_micro(yhi, same, other)[:, None],
        input_grad[:, None],
        *matrix_grads,
        heads[:, 0].reshape(-1),
        heads[:, 2].reshape(-1),
        own[2],
        pick(sums[6 * D : 7 * D].reshape(2, 1024), yhi),
        own[5],
        own[0],
        own[1],
        own[3],
        own[4],
    )


def solution(mesh):
    split = Mesh(mesh.devices.reshape(2, 2, 4, 2, 4), AXES)
    token = P(None, "core", ("ylo", "x"), None)
    inner = P(("core", "ylo", "x"), ("yhi", "z"))
    outer = P(("yhi", "z"), ("core", "ylo", "x"))
    unit = P(("yhi", "z"))
    matrix = (inner, inner, inner, outer, inner, outer)
    vector = (unit, unit, P(), unit, P(), P(), P(), P(), P())
    in_specs = (token, token, P(None, "core", None)) + matrix + vector
    out_specs = (token, token) + matrix + vector
    return jax.shard_map(shards, mesh=split, in_specs=in_specs, out_specs=out_specs, check_vma=False)
```
